128 devices in a mesh: grp: 8 (over x, core), dev: 16 (over y, z).
Axes of the slice: x: 4, y: 4, z: 4, core: 2. Of those that a mesh axis runs over, the one named last changes fastest.
Arguments:
- features: bfloat16 [2, 131072, 256], P(None, ('grp', 'dev')), may hold values from -6 to 6
- w_source: bfloat16 [256, 256], P('dev'), may hold values from -0.375 to 0.375
- w_target: bfloat16 [256, 256], P('dev'), may hold values from -0.375 to 0.375
- w_residual: bfloat16 [256, 256], P('dev'), may hold values from -0.375 to 0.375
- attention: bfloat16 [256], P('dev'), may hold values from -1.5 to 1.5
- out_bias: bfloat16 [256], P('dev'), may hold values from -3 to 3
- norm_gain: bfloat16 [256], P('dev'), may hold values from 0.5 to 1.5
- norm_shift: bfloat16 [256], P('dev'), may hold values from -1.796875 to 1.796875
- node_count: int32 [2, 128], P(None, ('grp', 'dev')), may hold values from 512 to 1024, as said below
- edge_src: int32 [2, 128, 128, 16], P(None, ('grp', 'dev')), may hold values from 0 to 1023, as said below
- edge_tgt: int32 [2, 128, 128, 16], P(None, ('grp', 'dev')), may hold values from -1 to 1023, as said below
- cotangent: bfloat16 [2, 131072, 256], P(None, ('grp', 'dev')), may hold values from -6 to 6
Outputs:
- output: bfloat16 [2, 131072, 256], P(None, ('grp', 'dev'))
- grad_features: bfloat16 [2, 131072, 256], P(None, ('grp', 'dev'))
- grad_w_source: float32 [256, 256], P('dev')
- grad_w_target: float32 [256, 256], P('dev')
- grad_w_residual: float32 [256, 256], P('dev')
- grad_attention: float32 [256], P('dev')
- grad_bias: float32 [256], P('dev')
- grad_gain: float32 [256], P('dev')
- grad_shift: float32 [256], P('dev')
The draws below stay inside these ranges and needn't reach their ends.
Inputs may be any that keep to these rules, and one draw needn't show every extreme that they name: `node_count`: in each micro-batch some device holds exactly 1024 live nodes. `edge_src`: entry [b, s, t, k] is below node_count[b, s]. `edge_tgt`: entry [b, t, s, k] is below node_count[b, t] for the first c slots, where c from s to t is 8 to 16 (each source device sends exactly 16 to some target device in each micro-batch), and -1 in the others.
All inputs are finite; a program needn't handle non-finite values.
Results may differ from the reference program's by a relative error of at most 0.0075.
Values may be sent and summed in bfloat16 or wider, within the bound.
A program may use at most 128 MiB of HBM per device.

```python
import jax
import jax.numpy as jnp
from jax import lax

D = 256
H = 4
NODE_DEV = 1024
CAP = 16
MB = 2
NODES = 131072
DEVICES = 128


def graph_counts(key):
    key_nodes, key_pairs, key_full, key_pick = jax.random.split(key, 4)
    node_totals = jax.random.randint(key_nodes, (MB, DEVICES), NODE_DEV // 2, NODE_DEV + 1)
    chosen = jax.random.randint(key_full, (MB, 1), 0, DEVICES)
    node_totals = jnp.where(jnp.arange(DEVICES)[None, :] == chosen, NODE_DEV, node_totals)
    pair_totals = jax.random.randint(key_pairs, (MB, DEVICES, DEVICES), CAP // 2, CAP + 1)
    picked = jax.random.randint(key_pick, (MB, DEVICES, 1), 0, DEVICES)
    pair_totals = jnp.where(jnp.arange(DEVICES)[None, None, :] == picked, CAP, pair_totals)
    return (node_totals.astype(jnp.int32), pair_totals.astype(jnp.int32))


def draw_node_count(key, part):
    node_totals, pair_totals = graph_counts(key)
    return node_totals


def draw_edge_src(key, part):
    node_totals, pair_totals = graph_counts(key)
    key = jax.random.fold_in(key, 5)
    drawn = jax.random.randint(key, (MB, DEVICES, DEVICES, CAP), 0, 1 << 20)
    return (drawn % node_totals[:, :, None, None]).astype(jnp.int32)


def draw_edge_tgt(key, part):
    node_totals, pair_totals = graph_counts(key)
    key = jax.random.fold_in(key, 9)
    drawn = jax.random.randint(key, (MB, DEVICES, DEVICES, CAP), 0, 1 << 20)
    picked = drawn % node_totals[:, :, None, None]
    incoming = jnp.transpose(pair_totals, (0, 2, 1))
    slot_ids = jnp.arange(CAP)[None, None, None, :]
    return jnp.where(slot_ids < incoming[:, :, :, None], picked, -1).astype(jnp.int32)


def block_levels(own_key, dims, pieces, least, largest):
    loudness, own = 1.0, jax.random.fold_in(own_key, 6)
    for axis_at, parts in pieces:
        draws = jnp.exp(jax.random.uniform(jax.random.fold_in(own, axis_at), (parts,), jnp.float32, least / len(pieces), largest / len(pieces)))
        loudness = loudness * jnp.repeat(draws, dims[axis_at] // parts).reshape([-1 if axis == axis_at else 1 for axis in range(len(dims))])
    return loudness


def centred(own_key, extent, width, reach, cuts=(), kind=jnp.bfloat16):
    values = jax.random.normal(own_key, extent, jnp.float32) * width
    if len(cuts) > 0:
        values = block_levels(own_key, extent, cuts, -0.22, 0.18) * values
    return jnp.clip(values, min=-reach, max=reach).astype(kind)


def setup_inputs(seed: int = 0) -> dict:
    key_of = jax.random.split(jax.random.key(seed), 13)
    features = centred(key_of[0], (MB, NODES, D), 1.0, 6.0, ((1, 128),))
    w_source = centred(key_of[1], (D, D), D ** -0.5, 0.375, ((0, 16),))
    w_target = centred(key_of[2], (D, D), D ** -0.5, 0.375, ((0, 16),))
    w_residual = centred(key_of[3], (D, D), D ** -0.5, 0.375, ((0, 16),))
    attention = centred(key_of[4], (D,), 0.25, 1.5, ((0, 16),))
    out_bias = centred(key_of[5], (D,), 0.5, 3.0, ((0, 16),))
    norm_gain = jnp.clip(1.0 + 0.1 * jax.random.normal(key_of[6], (D,), jnp.float32), 0.5, 1.5).astype(jnp.bfloat16)
    norm_shift = centred(key_of[7], (D,), 0.3, 1.796875, ((0, 16),))
    node_count = draw_node_count(jax.random.fold_in(key_of[12], 71), 0)
    edge_src = draw_edge_src(jax.random.fold_in(key_of[12], 71), 0)
    edge_tgt = draw_edge_tgt(jax.random.fold_in(key_of[12], 71), 0)
    cotangent = centred(key_of[11], (MB, NODES, D), 1.0, 6.0, ((1, 128),))
    return {"features": features, "w_source": w_source, "w_target": w_target, "w_residual": w_residual, "attention": attention, "out_bias": out_bias, "norm_gain": norm_gain, "norm_shift": norm_shift, "node_count": node_count, "edge_src": edge_src, "edge_tgt": edge_tgt, "cotangent": cotangent}


@jax.custom_vjp
def low(v):
    return lax.optimization_barrier(v.astype(jnp.bfloat16)).astype(jnp.float32)

@jax.custom_vjp
def low_back(v):
    return v

def low_keep(v):
    return (low(v), None)

def low_pass(kept, grad):
    return (grad,)

def back_keep(v):
    return (v, None)

def back_low(kept, grad):
    return (low(grad),)
low.defvjp(low_keep, low_pass)
low_back.defvjp(back_keep, back_low)

def matmul(left, right):
    return jnp.dot(left, right, precision=lax.Precision.HIGHEST)

def smooth_unit(value):
    return jax.nn.gelu(value, approximate=True)

def head_scores(summed, attn_vec):
    shaped = smooth_unit(summed).reshape(summed.shape[0], H, D // H)
    return lax.optimization_barrier(jnp.sum(shaped * attn_vec.reshape(H, D // H), axis=-1))

def reference(features, w_source, w_target, w_residual, attention, out_bias, norm_gain, norm_shift, node_count, edge_src, edge_tgt, cotangent):
    total_nodes = DEVICES * NODE_DEV
    head_width = D // H
    graphs = []
    for batch in range(MB):
        dev_ids = jnp.arange(DEVICES, dtype=jnp.int32)
        sources = (dev_ids[:, None, None] * NODE_DEV + edge_src[batch]).reshape(-1)
        tgt_local = jnp.transpose(edge_tgt[batch], (1, 0, 2))
        edge_live = (tgt_local >= 0).reshape(-1)
        targets = jnp.where(tgt_local >= 0, dev_ids[None, :, None] * NODE_DEV + tgt_local, total_nodes).reshape(-1).astype(jnp.int32)
        node_live = (jnp.arange(NODE_DEV, dtype=jnp.int32)[None, :] < node_count[batch][:, None]).reshape(-1)
        graphs.append((sources, targets, edge_live, node_live))

    def forward(feats, wsrc, wtgt, wres, attn_vec, bias_vec, gain_vec, shift_vec):
        results = []
        for batch in range(MB):
            sources, targets, edge_live, node_live = graphs[batch]
            rows = feats[batch]
            src_proj = low(low_back(matmul(rows, wsrc)))
            tgt_proj = low_back(matmul(rows, wtgt))
            res_proj = low_back(matmul(rows, wres))
            edge_rows = low_back(src_proj[sources])
            tgt_pad = jnp.concatenate([tgt_proj, jnp.zeros((1, D), jnp.float32)], 0)
            edge_score = head_scores(edge_rows + tgt_pad[targets], attn_vec)
            self_score = head_scores(src_proj + tgt_proj, attn_vec)
            masked = jnp.where(edge_live[:, None], edge_score, -jnp.inf)
            edge_top = jax.ops.segment_max(masked, targets, total_nodes + 1)[:total_nodes]
            top_score = jnp.maximum(edge_top, self_score)
            top_pad = jnp.concatenate([top_score, jnp.zeros((1, H), jnp.float32)], 0)
            edge_exp = jnp.exp(edge_score - top_pad[targets]) * edge_live[:, None].astype(jnp.float32)
            self_exp = jnp.exp(self_score - top_score)
            denom = jax.ops.segment_sum(edge_exp, targets, total_nodes + 1)[:total_nodes] + self_exp
            denom_pad = jnp.concatenate([denom, jnp.ones((1, H), jnp.float32)], 0)
            edge_alpha = edge_exp / denom_pad[targets]
            self_alpha = self_exp / denom
            edge_vals = edge_alpha[:, :, None] * edge_rows.reshape(-1, H, head_width)
            aggregate = jax.ops.segment_sum(edge_vals, targets, total_nodes + 1)[:total_nodes]
            aggregate = aggregate + self_alpha[:, :, None] * src_proj.reshape(-1, H, head_width)
            summed = aggregate.reshape(-1, D) + bias_vec + res_proj
            centre = summed - lax.optimization_barrier(jnp.mean(summed, axis=-1, keepdims=True))
            normed = centre * lax.rsqrt(lax.optimization_barrier(jnp.mean(centre * centre, axis=-1, keepdims=True)) + 1e-05)
            lin = normed * gain_vec + shift_vec
            results.append(jax.nn.elu(lin) * node_live[:, None].astype(jnp.float32))
        return jnp.stack(results)
    inputs = (features.astype(jnp.float32), w_source.astype(jnp.float32), w_target.astype(jnp.float32), w_residual.astype(jnp.float32), attention.astype(jnp.float32), out_bias.astype(jnp.float32), norm_gain.astype(jnp.float32), norm_shift.astype(jnp.float32))
    outcome, pullback = jax.vjp(forward, *inputs)
    grads = pullback(cotangent.astype(jnp.float32))
    return (outcome.astype(jnp.bfloat16), grads[0].astype(jnp.bfloat16), grads[1], grads[2], grads[3], grads[4], grads[5], grads[6], grads[7])
```

```python
import functools

import jax
import jax.numpy as jnp
from jax import lax
from jax.experimental import pallas as pl
from jax.experimental.pallas import tpu as pltpu
from jax.sharding import PartitionSpec as P

MESH = pl.DeviceIdType.MESH
BF = jnp.bfloat16
F32 = jnp.float32
H = 4
LOWEST = -1e30
C0 = 0.7978845608028654
C1 = 0.044715


def dot(a, b):
    return jnp.dot(a, b, preferred_element_type=F32)


def dot_nt(a, b):
    return lax.dot_general(a, b, (((1,), (1,)), ((), ())), preferred_element_type=F32)


def dot_tn(a, b):
    return lax.dot_general(a, b, (((0,), (0,)), ((), ())), preferred_element_type=F32)


def iota(shape, axis, kind=jnp.int32):
    return lax.broadcasted_iota(kind, shape, axis)


def gelu_pair(z):
    zz = z * z
    t = jnp.tanh(z * (C0 + (C0 * C1) * zz))
    half = 0.5 * z
    g = half + half * t
    gp = (0.5 + 0.5 * t) + (half - half * (t * t)) * (C0 + (3.0 * C0 * C1) * zz)
    return g, gp


def split(v):
    hi = v.astype(BF)
    return hi, (v - hi.astype(F32)).astype(BF)


def kernel(
    cfg,
    cnt_ref, esrc_ref, etgt_ref, att_ref, bias_ref, gain_ref, shift_ref,
    x_hbm, cot_hbm, ws_hbm, wt_hbm, wr_hbm,
    out_hbm, gf_hbm, small_ref,
    x_v, xt_v, cot_v, fs, fr, rs, rr, wsend, wall, wcat,
    tcolf, trow, srow, th, tht,
    se_v, g_v, ga_v, sc_v, pv_v, sp_v, tp_v, rp_v, sg_v, sga_v, ssc_v, mtab, mx_v,
    dtab, loc_v, a2, eblk, exp2, spread, sel, vecs, vacc, gacc,
    g0s, g0r, g1s, g1r, g2s, g2r,
    in_sem, fs_sem, fr_sem, rs_sem, rr_sem, w_sem, r_sem, out_sem,
):
    NG, ND, X, Y, Z, N, CAP, MB, EC = cfg
    C = 256
    DEV = NG * ND
    E = DEV * CAP
    NCH = E // EC
    PER = EC // CAP
    RW = C // ND
    PK = 3 * RW + 16
    HALF = PK // 2
    NB = min(256, N)
    W8 = 2 * X
    g, d = lax.axis_index("grp"), lax.axis_index("dev")
    mx, mc = lax.div(g, 2), lax.rem(g, 2)
    my, mz = lax.div(d, Z), lax.rem(d, Z)
    twin = (mx * 2 + 1 - mc, d)

    def place(i, q, sign):
        a, k = q // 2, q % 2
        if isinstance(i, int):
            b, c = i % Y, i // Y
            dy, dz = (a + b) % Y, (a + b + c) % Z
        else:
            b, c = lax.rem(i, Y), lax.div(i, Y)
            dy, dz = lax.rem(a + b, Y), lax.rem(a + b + c, Z)
        if sign > 0:
            px, py, pz = mx + a, my + dy, mz + dz
        else:
            px, py, pz = mx + (X - a), my + (Y - dy), mz + (Z - dz)
        return (
            lax.rem(px, X) * 2 + lax.rem(mc + k, 2),
            lax.rem(py, Y) * Z + lax.rem(pz, Z),
        )

    barrier = pltpu.get_barrier_semaphore()

    def greet(i, q):
        pl.semaphore_signal(barrier, inc=1, device_id=place(i, q, 1), device_id_type=MESH)

    def greet_all(i, carry):
        for q in range(W8):
            greet(i, q)
        return carry

    for q in range(1, W8):
        greet(0, q)
    lax.fori_loop(1, DEV // W8, greet_all, 0)
    loads = [
        pltpu.make_async_copy(x_hbm, x_v, in_sem.at[0]),
        pltpu.make_async_copy(ws_hbm, wsend.at[pl.ds(0, RW)], in_sem.at[1]),
        pltpu.make_async_copy(wt_hbm, wsend.at[pl.ds(RW, RW)], in_sem.at[2]),
        pltpu.make_async_copy(wr_hbm, wsend.at[pl.ds(2 * RW, RW)], in_sem.at[3]),
        pltpu.make_async_copy(cot_hbm, cot_v, in_sem.at[4]),
    ]
    for load in loads:
        load.start()

    rep = (iota((RW, C), 1) % RW == iota((RW, C), 0)).astype(F32).astype(BF)
    here = (iota((8, C), 1) // RW == d)
    rows = [jnp.where(here, dot(jnp.broadcast_to(ref[...], (8, RW)), rep), 0.0)
            for ref in (att_ref, bias_ref, gain_ref, shift_ref)]
    line = iota((8, C), 0)
    placed = jnp.zeros((8, C), F32)
    for slot in range(4):
        placed = jnp.where(line == slot, rows[slot], placed)
    wsend[pl.ds(3 * RW, 16), :] = jnp.concatenate([placed, jnp.zeros((8, C), F32)], axis=0).astype(BF)

    def order(sign):
        j = iota((DEV, DEV), 0)
        k = j & 1
        a = (j >> 1) & (X - 1)
        b = (j // W8) & (Y - 1)
        c = j // (W8 * Y)
        dx, dy, dz = a, (a + b) & (Y - 1), (a + b + c) & (Z - 1)
        px = (mx + X + sign * dx) & (X - 1)
        py = (my + Y + sign * dy) & (Y - 1)
        pz = (mz + Z + sign * dz) & (Z - 1)
        dev = (px * 2 + ((mc + k) & 1)) * ND + py * Z + pz
        return (dev == iota((DEV, DEV), 1)).astype(F32).astype(BF)

    TC = min(E, 256)
    LB = 2 * CAP
    lists = []
    for sign, tabs in ((1, esrc_ref), (-1, etgt_ref)):
        perm = order(sign)
        for mb in range(MB):
            parts = jnp.concatenate([tabs[mb, 0] >> 5, tabs[mb, 0] & 31], axis=0)
            lists.append(dot_nt(perm, parts.astype(F32).astype(BF)))
    packed = jnp.concatenate(lists, axis=1).astype(BF)
    LW = 2 * MB * LB
    lane = iota((LW, 2 * MB * 128), 0)
    scale = jnp.where((lane & (LB - 1)) < CAP, 32.0, 1.0)
    widen = jnp.where((lane // LB) == (iota((LW, 2 * MB * 128), 1) // 128), scale, 0.0).astype(BF)
    lane = iota((2 * MB * 16, LW), 1)
    scale = jnp.where((lane & (LB - 1)) < CAP, 32.0, 1.0)
    turn = jnp.where((lane // LB) == (iota((2 * MB * 16, LW), 0) // 16), scale, 0.0).astype(BF)

    def onehot_rows(col):
        wide = jnp.concatenate([col] * (N // 128), axis=1)
        return jnp.where(wide == iota(wide.shape, 1, jnp.int16), jnp.ones((), BF), jnp.zeros((), BF))

    def list_step(i, carry):
        r = pl.multiple_of(i * TC, TC)
        e = iota((TC, DEV), 0) + r
        pairs = ((e // CAP) == iota((TC, DEV), 1)).astype(F32).astype(BF)
        own = (iota((TC, LW), 0) & (CAP - 1)) == (iota((TC, LW), 1) & (CAP - 1))
        kept = jnp.where(own, dot(pairs, packed), 0.0).astype(BF)
        wide = dot(kept, widen)
        flat = dot_nt(turn, kept).astype(jnp.int32).astype(jnp.int16)
        for mb in range(MB):
            out = wide[:, mb * 128:(mb + 1) * 128].astype(jnp.int32).astype(jnp.int16)
            fs[mb, pl.ds(r, TC), :] = dot(onehot_rows(out), x_v[mb]).astype(BF)
            part = wide[:, (MB + mb) * 128:(MB + mb + 1) * 128]
            tcolf[mb, pl.ds(r, TC), :] = part
            th[mb, pl.ds(r, TC), :] = onehot_rows(part.astype(jnp.int32).astype(jnp.int16))
            srow[mb, i] = flat[mb * 16:(mb + 1) * 16, :]
            trow[mb, i] = flat[(MB + mb) * 16:(MB + mb + 1) * 16, :]
        return carry

    loads[0].wait()
    lax.fori_loop(0, E // TC, list_step, 0)

    def fill_turned(row, mb, dst):
        def step(i, carry):
            r = pl.multiple_of(i * 128, 128)
            ids = iota((128, TC), 0, jnp.int16) + (i * 128).astype(jnp.int16)
            for q in range(E // TC):
                wide = jnp.concatenate([row[mb, q]] * 8, axis=0)
                dst[mb, pl.ds(r, 128), q * TC:(q + 1) * TC] = jnp.where(
                    wide == ids, jnp.ones((), BF), jnp.zeros((), BF)
                )
            return carry

        lax.fori_loop(0, N // 128, step, 0)

    for mb in range(MB):
        fill_turned(trow, mb, tht)
    for load in loads[1:4]:
        load.wait()

    pl.semaphore_wait(barrier, DEV - 1)

    half = pl.ds(pl.multiple_of(mc * HALF, 16), HALF)

    def send_weights(i, carry):
        pltpu.make_async_remote_copy(
            src_ref=wsend.at[half], dst_ref=wall.at[d, half],
            send_sem=w_sem.at[0], recv_sem=w_sem.at[1],
            device_id=(g, lax.rem(d + i, ND)), device_id_type=MESH,
        ).start()
        return carry

    lax.fori_loop(1, ND, send_weights, 0)
    pltpu.make_async_copy(wsend.at[half], wall.at[d, half], w_sem.at[1]).start()

    def send_block(src, dst, mb, i, q, sign, ssem, rsem):
        rows = pl.ds(pl.multiple_of((i * W8 + q) * CAP, CAP), CAP)
        chunk = i * W8 // PER if isinstance(i, int) else lax.div(i, PER // W8)
        pltpu.make_async_remote_copy(
            src_ref=src.at[mb, rows], dst_ref=dst.at[mb, rows],
            send_sem=ssem.at[mb], recv_sem=rsem.at[mb, chunk],
            device_id=place(i, q, sign), device_id_type=MESH,
        ).start()

    def keep_block(src, dst, mb, rsem):
        pltpu.make_async_copy(
            src.at[mb, pl.ds(0, CAP)], dst.at[mb, pl.ds(0, CAP)], rsem.at[mb, 0]
        ).start()

    def send_rows(mb, carry):
        keep_block(fs, fr, mb, fr_sem)
        for q in range(1, W8):
            send_block(fs, fr, mb, 0, q, 1, fs_sem, fr_sem)

        def more(i, carry):
            for q in range(W8):
                send_block(fs, fr, mb, i, q, 1, fs_sem, fr_sem)
            return carry

        lax.fori_loop(1, DEV // W8, more, 0)
        return carry

    lax.fori_loop(0, MB, send_rows, 0)

    for mb in range(MB):
        for i in range(N // 128):
            xt_v[mb, :, i * 128:(i + 1) * 128] = jnp.transpose(x_v[mb, i * 128:(i + 1) * 128, :])

    same = (iota((C, C), 0) // 64) == (iota((C, C), 1) // 64)
    eblk[...] = same.astype(F32).astype(BF)
    lane = iota((128, C), 0)
    head = iota((128, C), 1) // 64
    exp2[...] = ((lane < 8) & ((lane & 3) == head)).astype(F32).astype(BF)
    groups = N // 64
    r = lane & 63
    at = 2 * ((r & 31) // groups) + r // 32
    spread[...] = ((at == head) & ((r & 31) < 2 * groups)).astype(F32).astype(BF)
    pick = iota((C, 128), 0)
    slot = iota((C, 128), 1)
    sel[0] = ((pick == 64 * slot) & (slot < 4)).astype(F32).astype(BF)
    sel[1] = ((pick == 64 * (slot - 4)) & (slot >= 4) & (slot < 8)).astype(F32).astype(BF)
    vacc[...] = jnp.zeros_like(vacc)
    gacc[...] = jnp.zeros_like(gacc)

    mine = wall.at[:, half]
    pltpu.make_async_copy(mine, mine, w_sem.at[1]).wait()
    pltpu.make_async_remote_copy(
        src_ref=mine, dst_ref=mine, send_sem=w_sem.at[2], recv_sem=w_sem.at[3],
        device_id=twin, device_id_type=MESH,
    ).start()
    pltpu.make_async_copy(mine, mine, w_sem.at[3]).wait()
    for slot in range(3):
        wcat[:, slot * C:(slot + 1) * C] = wall[:, slot * RW:(slot + 1) * RW, :].reshape(C, C)
    vectors = jnp.sum(wall[:, 3 * RW:3 * RW + 16, :].astype(F32), axis=0)
    vecs[...] = vectors[0:8, :]
    att_col = jnp.transpose(jnp.broadcast_to(vecs[0:1, :], (C, C)))
    a2[...] = jnp.where(same, att_col, 0.0).astype(BF)

    def project(i, carry):
        mb, part = lax.div(i, N // NB), lax.rem(i, N // NB)
        rows = pl.ds(pl.multiple_of(part * NB, NB), NB)
        proj = dot(x_v[mb, rows, :], wcat[...])
        sp = proj[:, 0:C].astype(BF)
        tp = proj[:, C:2 * C]
        sp_v[mb, rows, :] = sp
        tp_v[mb, rows, :] = tp.astype(BF)
        rp_v[mb, rows, :] = proj[:, 2 * C:3 * C]
        gs, gp = gelu_pair(sp.astype(F32) + tp)
        hi, lo = split(gs)
        sg_v[mb, rows, :] = hi
        sga_v[mb, rows, :] = gp * vecs[0:1, :]
        ssc_v[mb, rows, :] = dot(hi, a2[...]) + dot(lo, a2[...])
        return carry

    lax.fori_loop(0, MB * (N // NB), project, 0)
    loads[4].wait()

    def fold(v):
        return jnp.sum(v.reshape(v.shape[0] // 8, 8, v.shape[1]), axis=0)

    def edge_rows(i):
        return slice(i * EC, (i + 1) * EC)

    def score_chunk(mb, i):
        rows = edge_rows(i)
        part = fr.at[mb, pl.ds(i * EC, EC)]
        pltpu.make_async_copy(part, part, fr_sem.at[mb, i]).wait()
        se = dot(fr[mb, rows, :], wcat[:, 0:C]).astype(BF)
        se_v[rows, :] = se
        z = se.astype(F32) + dot(th[mb, rows, :], tp_v[mb])
        ge, gp = gelu_pair(z)
        hi, lo = split(ge)
        g_v[rows, :] = hi
        ga_v[rows, :] = gp * vecs[0:1, :]
        sc_v[rows, :] = dot(hi, a2[...]) + dot(lo, a2[...])

    def sweep_chunk(mb, i):
        low = (iota((128, 128), 1) & 63).astype(F32)
        for q in range(EC // 128):
            part = slice(i * EC + q * 128, i * EC + (q + 1) * 128)
            tgt = tcolf[mb, part, :]
            s0, s1 = sc_v[part, 0:128], sc_v[part, 128:256]
            for grp in range(groups):
                hit = tgt == low + (64.0 * grp)
                for side, s in enumerate((s0, s1)):
                    top = jnp.max(jnp.where(hit, s, LOWEST).reshape(16, 8, 128), axis=0)
                    at = side * groups + grp
                    mx_v[at] = jnp.maximum(mx_v[at], top)

    def forward_edges(mb):
        mx_v[...] = jnp.full(mx_v.shape, LOWEST, F32)
        for i in range(NCH):
            score_chunk(mb, i)
            if i > 0:
                sweep_chunk(mb, i - 1)
        sweep_chunk(mb, NCH - 1)

    def tops(mb):
        best = jnp.max(mx_v[...], axis=1)
        best = jnp.concatenate([best, jnp.zeros((128 - 2 * groups, 128), F32)], axis=0)
        turned = jnp.transpose(best)
        both = turned[0:64, :] + pltpu.roll(turned[64:128, :], 32, 1)
        hi = both.astype(BF).astype(F32)
        table = hi + pltpu.roll(both - hi, 64, 1)
        for i in range(N // NB):
            rows = slice(i * NB, (i + 1) * NB)
            whose = iota((NB, 128), 0) // 64 + i * (NB // 64)
            mine = jnp.concatenate([table] * (NB // 64), axis=0)
            mine = jnp.where((iota((NB, 128), 1) & (groups - 1)) == whose, mine, 0.0).astype(BF)
            own = ssc_v[mb, rows, :]
            hi, lo = split(jnp.maximum(dot(mine, spread[...]), own))
            ssc_v[mb, rows, :] = jnp.exp(own - (hi.astype(F32) + lo.astype(F32)))
            mtab[rows, :] = (dot(hi, sel[0]) + dot(lo, sel[1])).astype(BF)

    def weigh(mb):
        for i in range(NCH):
            rows = edge_rows(i)
            me = dot(th[mb, rows, :], mtab[...]).astype(BF)
            live = tcolf[mb, rows, :] >= 0.0
            live = jnp.concatenate([live, live], axis=1)
            p = jnp.where(live, jnp.exp(sc_v[rows, :] - dot(me, exp2[...])), 0.0)
            pv_v[rows, 0:C] = (p * se_v[rows, :].astype(F32)).astype(BF)
            pv_v[rows, C:2 * C] = p.astype(BF)

    def nodes(mb):
        for i in range(N // NB):
            rows = slice(i * NB, (i + 1) * NB)
            sc_v[rows, :] = dot(tht[mb, rows, :], pv_v[:, 0:C])
            sc_v[N + i * NB:N + (i + 1) * NB, :] = dot(tht[mb, rows, :], pv_v[:, C:2 * C])
        for i in range(N // NB):
            r = i * NB
            rows = slice(r, r + NB)
            ps = ssc_v[mb, rows, :]
            inv = 1.0 / (sc_v[N + r:N + r + NB, :] + ps)
            sp = sp_v[mb, rows, :].astype(F32)
            agg = (sc_v[rows, :] + ps * sp) * inv
            alpha = ps * inv
            live = (iota((NB, 1), 0) + r < cnt_ref[0, mb]).astype(F32)
            pre = agg + vecs[1:2, :] + rp_v[mb, rows, :]
            centre = pre - jnp.mean(pre, axis=1, keepdims=True)
            rstd = lax.rsqrt(jnp.mean(centre * centre, axis=1, keepdims=True) + 1e-05)
            nrm = centre * rstd
            lin = nrm * vecs[2:3, :] + vecs[3:4, :]
            e = jnp.exp(jnp.minimum(lin, 0.0))
            up = lin > 0
            x_v2 = jnp.where(up, lin, e - 1.0) * live
            cot = cot_v[mb, rows, :].astype(F32) * live
            cot_v[mb, rows, :] = x_v2.astype(BF)
            dlin = cot * jnp.where(up, 1.0, e)
            vacc[2] += fold(dlin * nrm)
            vacc[3] += fold(dlin)
            dn = dlin * vecs[2:3, :]
            dpre = rstd * (
                dn
                - jnp.mean(dn, axis=1, keepdims=True)
                - nrm * jnp.mean(dn * nrm, axis=1, keepdims=True)
            )
            vacc[1] += fold(dpre)
            loc_v[mb, rows, 2 * C:3 * C] = dpre.astype(BF)
            dagr = (dpre * inv).astype(BF)
            dagf = dagr.astype(F32)
            hi, lo = split(dagf * agg)
            big = dot(hi, eblk[...]) + dot(lo, eblk[...])
            hi, lo = split(dagf * (sp - agg))
            ds = ps * (dot(hi, eblk[...]) + dot(lo, eblk[...]))
            vacc[0] += fold(ds * sg_v[mb, rows, :].astype(F32))
            dz = ds * sga_v[mb, rows, :].astype(F32)
            loc_v[mb, rows, C:2 * C] = dz.astype(BF)
            loc_v[mb, rows, 0:C] = (alpha * dpre + dz).astype(BF)
            dtab[rows, 0:C] = dagr
            hi, lo = split(big)
            dtab[rows, C:C + 128] = (dot(hi, sel[0]) + dot(lo, sel[1])).astype(BF)

    def grad_chunk(mb, i):
        rows = edge_rows(i)
        got = dot(th[mb, rows, :], dtab[...])
        dag = got[:, 0:C]
        se = se_v[rows, :].astype(F32)
        hi, lo = split(dag * se)
        p = pv_v[rows, C:2 * C].astype(F32)
        ds = p * (dot(hi, eblk[...]) + dot(lo, eblk[...]) - dot(got[:, C:C + 128].astype(BF), exp2[...]))
        vacc[0] += fold(ds * g_v[rows, :].astype(F32))
        dz = ds * ga_v[rows, :]
        eg = (p * dag + dz).astype(BF)
        rs[mb, rows, :] = eg
        gacc[:, 0:C] += dot_tn(fr[mb, rows, :], eg)
        fr[mb, rows, :] = dz.astype(BF)

    def return_chunk(mb, i):
        if i == 0:
            keep_block(rs, rr, mb, rr_sem)
        for j in range(max(1, i * PER), (i + 1) * PER):
            send_block(rs, rr, mb, j // W8, j % W8, -1, rs_sem, rr_sem)

    def backward_edges(mb):
        for i in range(NCH):
            grad_chunk(mb, i)
            if i > 0:
                return_chunk(mb, i - 1)
        return_chunk(mb, NCH - 1)

    def one_batch(mb, carry):
        forward_edges(mb)
        tops(mb)
        weigh(mb)
        nodes(mb)
        pltpu.make_async_copy(cot_v.at[mb], out_hbm.at[mb], out_sem.at[mb]).start()
        backward_edges(mb)
        return carry

    lax.fori_loop(0, MB, one_batch, 0)

    def local_grads(mb, carry):
        for i in range(N // NB):
            rows = slice(i * NB, (i + 1) * NB)
            dtgt = dot(tht[mb, rows, :], fr[mb]) + loc_v[mb, rows, C:2 * C].astype(F32)
            loc_v[mb, rows, C:2 * C] = dtgt.astype(BF)
        gacc[...] += dot(xt_v[mb], loc_v[mb])
        return carry

    lax.fori_loop(0, MB, local_grads, 0)

    def pack_vectors(v):
        hi = v.astype(BF).astype(F32)
        return jnp.concatenate([hi, v - hi], axis=0).astype(BF)

    def repack(v):
        cut = HALF - 16
        both = v[..., cut:cut + 8, :] + v[..., cut + 8:cut + 16, :]
        hi = both.astype(BF).astype(F32)
        last = jnp.concatenate([hi, both - hi], axis=-2)
        last = jnp.where(mc == 1, last, v[..., cut:cut + 16, :])
        return jnp.concatenate([v[..., 0:cut, :], last], axis=-2).astype(BF)

    for slot in range(3):
        g0s[:, slot * RW:(slot + 1) * RW, :] = gacc[:, slot * C:(slot + 1) * C].astype(BF).reshape(ND, RW, C)
    sums = [jnp.sum(vacc[slot], axis=0, keepdims=True) for slot in range(4)]
    packed = pack_vectors(jnp.concatenate(sums + [jnp.zeros((4, C), F32)], axis=0))
    for slot in range(ND):
        g0s[slot, 3 * RW:3 * RW + 16, :] = packed
    other = pl.ds(pl.multiple_of((1 - mc) * HALF, 16), HALF)
    pltpu.make_async_remote_copy(
        src_ref=g0s.at[:, other], dst_ref=g0r, send_sem=r_sem.at[4], recv_sem=r_sem.at[5],
        device_id=twin, device_id_type=MESH,
    ).start()

    def partials(mb, carry):
        for i in range(N // NB):
            rows = slice(i * NB, (i + 1) * NB)
            rp_v[mb, rows, :] = dot_nt(loc_v[mb, rows, C:3 * C], wcat[:, C:3 * C])
        fill_turned(srow, mb, tht)
        return carry

    partials(0, 0)
    pltpu.make_async_copy(g0r, g0r, r_sem.at[5]).wait()
    g1s[...] = repack(g0s[:, half, :].astype(F32) + g0r[...].astype(F32))

    def send_first(i, carry):
        to = lax.rem(d + i, ND)
        pltpu.make_async_remote_copy(
            src_ref=g1s.at[to], dst_ref=g1r.at[d], send_sem=r_sem.at[0], recv_sem=r_sem.at[1],
            device_id=(g, to), device_id_type=MESH,
        ).start()
        return carry

    lax.fori_loop(1, ND, send_first, 0)
    pltpu.make_async_copy(g1s.at[d], g1r.at[d], r_sem.at[1]).start()
    partials(1, 0)

    def finish(mb):
        for i in range(NCH):
            rows = pl.ds(i * EC, EC)
            pltpu.make_async_copy(rr.at[mb, rows], rr.at[mb, rows], rr_sem.at[mb, i]).wait()
        pltpu.make_async_copy(cot_v.at[mb], out_hbm.at[mb], out_sem.at[mb]).wait()

        def step(i, carry):
            rows = pl.ds(pl.multiple_of(i * NB, NB), NB)
            dsrc = (dot(tht[mb, rows, :], rr[mb]) + loc_v[mb, rows, 0:C].astype(F32)).astype(BF)
            cot_v[mb, rows, :] = (dot_nt(dsrc, wcat[:, 0:C]) + rp_v[mb, rows, :]).astype(BF)
            return carry

        lax.fori_loop(0, N // NB, step, 0)
        pltpu.make_async_copy(cot_v.at[mb], gf_hbm.at[mb], out_sem.at[mb]).start()

    finish(0)

    pltpu.make_async_copy(g1r, g1r, r_sem.at[1]).wait()
    g2s[...] = repack(jnp.sum(g1r[...].astype(F32), axis=0))

    def send_second(i, carry):
        pltpu.make_async_remote_copy(
            src_ref=g2s, dst_ref=g2r.at[g], send_sem=r_sem.at[2], recv_sem=r_sem.at[3],
            device_id=(lax.rem(g + i, NG), d), device_id_type=MESH,
        ).start()
        return carry

    lax.fori_loop(1, NG, send_second, 0)
    pltpu.make_async_copy(g2s, g2r.at[g], r_sem.at[3]).start()

    for mb in range(1, MB):
        finish(mb)

    pltpu.make_async_copy(g2r, g2r, r_sem.at[3]).wait()
    for side in range(2):
        total = g2r[side].astype(F32)
        for slot in range(1, X):
            total = total + g2r[2 * slot + side].astype(F32)
        small_ref[side * HALF:(side + 1) * HALF, :] = total
    tail = small_ref[3 * RW:3 * RW + 8, :] + small_ref[3 * RW + 8:3 * RW + 16, :]
    small_ref[3 * RW:3 * RW + 8, :] = pltpu.roll(tail, lax.rem(C - d * RW, C), 1)

    for mb in range(MB):
        pltpu.make_async_copy(cot_v.at[mb], gf_hbm.at[mb], out_sem.at[mb]).wait()
        most = pl.ds(0, (DEV - 1) * CAP)
        pltpu.make_async_copy(fs.at[mb, most], fs.at[mb, most], fs_sem.at[mb]).wait()
        pltpu.make_async_copy(rs.at[mb, most], rs.at[mb, most], rs_sem.at[mb]).wait()
    pltpu.make_async_copy(mine, mine, w_sem.at[2]).wait()
    others = pl.ds(0, ND - 1)
    mine = wall.at[others, half]
    pltpu.make_async_copy(mine, mine, w_sem.at[0]).wait()
    pltpu.make_async_copy(g0r, g0r, r_sem.at[4]).wait()
    pltpu.make_async_copy(g1s.at[others], g1s.at[others], r_sem.at[0]).wait()
    others = pl.ds(0, NG - 1)
    pltpu.make_async_copy(g2r.at[others], g2r.at[others], r_sem.at[2]).wait()


def hand_on(RW, out_in, gf_in, small_in, out_hbm, gf_hbm, gws, gwt, gwr, v0, v1, v2, v3, held, sems):
    MB = out_in.shape[0]
    loads, stores = [], []
    for mb in range(MB):
        for src, dst in ((out_in, out_hbm), (gf_in, gf_hbm)):
            slot = len(loads)
            loads.append(pltpu.make_async_copy(src.at[mb], held.at[slot], sems.at[0, slot]))
            stores.append(pltpu.make_async_copy(held.at[slot], dst.at[mb], sems.at[1, slot]))
    for load in loads:
        load.start()
    for slot, dst in enumerate((gws, gwt, gwr)):
        dst[...] = small_in[slot * RW:(slot + 1) * RW, :]
    for slot, dst in enumerate((v0, v1, v2, v3)):
        dst[...] = small_in[3 * RW + slot:3 * RW + slot + 1, 0:RW]
    for load, store in zip(loads, stores):
        load.wait()
        store.start()
    for store in stores:
        store.wait()


def local(
    shape,
    features, w_source, w_target, w_residual, attention, out_bias, norm_gain, norm_shift,
    node_count, edge_src, edge_tgt, cotangent,
):
    NG, ND = shape
    X = NG // 2
    Y = 1
    while Y * Y < ND:
        Y *= 2
    Z = ND // Y
    MB, N, C = features.shape
    CAP = edge_src.shape[3]
    DEV = NG * ND
    E = DEV * CAP
    EC = min(256, E // 2)
    NCH = E // EC
    RW = C // ND
    PK = 3 * RW + 16
    groups = N // 64
    TC = min(E, 256)
    vmem = pl.BlockSpec(memory_space=pltpu.VMEM)
    hbm = pl.BlockSpec(memory_space=pl.ANY)
    smem = pl.BlockSpec(memory_space=pltpu.SMEM)
    cfg = (NG, ND, X, Y, Z, N, CAP, MB, EC)
    V = pltpu.VMEM
    DMA = pltpu.SemaphoreType.DMA
    I16 = jnp.int16
    wide = jax.ShapeDtypeStruct((MB, N, C), BF)
    block = jax.ShapeDtypeStruct((RW, C), F32)
    line = jax.ShapeDtypeStruct((1, RW), F32)
    result, grad_rows, small = pl.pallas_call(
        functools.partial(kernel, cfg),
        out_shape=(wide, wide, jax.ShapeDtypeStruct((PK, C), F32)),
        in_specs=[smem] + [vmem] * 6 + [hbm] * 5,
        out_specs=(hbm, hbm, vmem),
        scratch_shapes=[
            V((MB, N, C), BF), V((MB, C, N), BF), V((MB, N, C), BF),
            V((MB, E, C), BF), V((MB, E, C), BF), V((MB, E, C), BF), V((MB, E, C), BF),
            V((PK, C), BF), V((ND, PK, C), BF), V((C, 3 * C), BF),
            V((MB, E, 128), F32),
            V((MB, E // TC, 16, TC), I16), V((MB, E // TC, 16, TC), I16),
            V((MB, E, N), BF), V((MB, N, E), BF),
            V((E, C), BF), V((E, C), BF), V((E, C), F32), V((max(E, 2 * N), C), F32), V((E, 2 * C), BF),
            V((MB, N, C), BF), V((MB, N, C), BF), V((MB, N, C), F32),
            V((MB, N, C), BF), V((MB, N, C), F32), V((MB, N, C), F32),
            V((N, 128), BF), V((2 * groups, 8, 128), F32),
            V((N, C + 128), BF), V((MB, N, 3 * C), BF),
            V((C, C), BF), V((C, C), BF), V((128, C), BF), V((128, C), BF), V((2, C, 128), BF),
            V((8, C), F32), V((4, 8, C), F32), V((C, 3 * C), F32),
            V((ND, PK, C), BF), V((ND, PK // 2, C), BF), V((ND, PK // 2, C), BF),
            V((ND, PK // 2, C), BF), V((PK // 2, C), BF), V((NG, PK // 2, C), BF),
            DMA((5,)), DMA((MB,)), DMA((MB, NCH)), DMA((MB,)), DMA((MB, NCH)),
            DMA((4,)), DMA((6,)), DMA((MB,)),
        ],
        compiler_params=pltpu.CompilerParams(
            collective_id=0, has_side_effects=True, vmem_limit_bytes=62 * 2**20
        ),
        cost_estimate=pl.CostEstimate(
            flops=20 * MB * E * N * C, bytes_accessed=10 * MB * N * C, transcendentals=4 * MB * E * C
        ),
    )(
        jnp.swapaxes(node_count, 0, 1), jnp.swapaxes(edge_src, 2, 3), jnp.swapaxes(edge_tgt, 2, 3),
        attention.reshape(1, RW), out_bias.reshape(1, RW), norm_gain.reshape(1, RW), norm_shift.reshape(1, RW),
        features, cotangent, w_source, w_target, w_residual,
    )
    outs = pl.pallas_call(
        functools.partial(hand_on, RW),
        out_shape=(wide, wide, block, block, block, line, line, line, line),
        in_specs=[hbm, hbm, vmem],
        out_specs=(hbm, hbm) + (vmem,) * 7,
        scratch_shapes=[V((2 * MB, N, C), BF), DMA((2, 2 * MB))],
    )(result, grad_rows, small)
    return outs[:5] + tuple(v.reshape(RW) for v in outs[5:])


def solution(mesh):
    shape = (mesh.shape["grp"], mesh.shape["dev"])
    return jax.shard_map(
        functools.partial(local, shape),
        mesh=mesh,
        in_specs=(
            P(None, ("grp", "dev"), None),
            P("dev", None),
            P("dev", None),
            P("dev", None),
            P("dev"),
            P("dev"),
            P("dev"),
            P("dev"),
            P(None, ("grp", "dev")),
            P(None, ("grp", "dev"), None, None),
            P(None, ("grp", "dev"), None, None),
            P(None, ("grp", "dev"), None),
        ),
        out_specs=(
            P(None, ("grp", "dev"), None),
            P(None, ("grp", "dev"), None),
            P("dev", None),
            P("dev", None),
            P("dev", None),
            P("dev"),
            P("dev"),
            P("dev"),
            P("dev"),
        ),
        check_vma=False,
    )
```

```python
import functools

import jax
import jax.numpy as jnp
from jax import lax
from jax.experimental import pallas as pl
from jax.experimental.pallas import tpu as pltpu
from jax.sharding import PartitionSpec as P

MESH = pl.DeviceIdType.MESH
BF = jnp.bfloat16
F32 = jnp.float32
H = 4
LOWEST = -1e30
C0 = 0.7978845608028654
C1 = 0.044715


def dot(a, b):
    return jnp.dot(a, b, preferred_element_type=F32)


def dot_nt(a, b):
    return lax.dot_general(a, b, (((1,), (1,)), ((), ())), preferred_element_type=F32)


def dot_tn(a, b):
    return lax.dot_general(a, b, (((0,), (0,)), ((), ())), preferred_element_type=F32)


def iota(shape, axis, kind=jnp.int32):
    return lax.broadcasted_iota(kind, shape, axis)


def gelu_pair(z):
    zz = z * z
    t = jnp.tanh(z * (C0 + (C0 * C1) * zz))
    half = 0.5 * z
    g = half + half * t
    gp = (0.5 + 0.5 * t) + (half - half * (t * t)) * (C0 + (3.0 * C0 * C1) * zz)
    return g, gp


def split(v):
    hi = v.astype(BF)
    return hi, (v - hi.astype(F32)).astype(BF)


def kernel(
    cfg,
    cnt_ref, esrc_ref, etgt_ref, att_ref, bias_ref, gain_ref, shift_ref,
    x_hbm, cot_hbm, ws_hbm, wt_hbm, wr_hbm,
    out_hbm, gf_hbm, small_ref,
    x_v, xt_v, cot_v, fs, fr, rs, rr, wsend, wall, wcat,
    lists, tcolf, trow, srow, th, tht,
    se_v, g_v, ga_v, sc_v, pv_v, sp_v, tp_v, rp_v, sg_v, sga_v, ssc_v, mtab, mx_v,
    dtab, loc_v, a2, eblk, exp2, spread, sel, vecs, vacc, gacc,
    g0s, g0r, g1s, g1r, g2s, g2r,
    in_sem, fs_sem, fr_sem, rs_sem, rr_sem, w_sem, r_sem, out_sem,
):
    NG, ND, X, Y, Z, N, CAP, MB, EC = cfg
    C = 256
    DEV = NG * ND
    E = DEV * CAP
    NCH = E // EC
    PER = EC // CAP
    RW = C // ND
    PK = 3 * RW + 16
    HALF = PK // 2
    NB = min(256, N)
    W8 = 2 * X
    g, d = lax.axis_index("grp"), lax.axis_index("dev")
    mx, mc = lax.div(g, 2), lax.rem(g, 2)
    my, mz = lax.div(d, Z), lax.rem(d, Z)
    twin = (mx * 2 + 1 - mc, d)

    def place(i, q, sign):
        a, k = q // 2, q % 2
        if isinstance(i, int):
            b, c = i % Y, i // Y
            dy, dz = (a + b) % Y, (a + b + c) % Z
        else:
            b, c = lax.rem(i, Y), lax.div(i, Y)
            dy, dz = lax.rem(a + b, Y), lax.rem(a + b + c, Z)
        if sign > 0:
            px, py, pz = mx + a, my + dy, mz + dz
        else:
            px, py, pz = mx + (X - a), my + (Y - dy), mz + (Z - dz)
        return (
            lax.rem(px, X) * 2 + lax.rem(mc + k, 2),
            lax.rem(py, Y) * Z + lax.rem(pz, Z),
        )

    barrier = pltpu.get_barrier_semaphore()

    def greet(i, q):
        pl.semaphore_signal(barrier, inc=1, device_id=place(i, q, 1), device_id_type=MESH)

    def greet_all(i, carry):
        for q in range(W8):
            greet(i, q)
        return carry

    for q in range(1, W8):
        greet(0, q)
    lax.fori_loop(1, DEV // W8, greet_all, 0)
    loads = [
        pltpu.make_async_copy(x_hbm, x_v, in_sem.at[0]),
        pltpu.make_async_copy(ws_hbm, wsend.at[pl.ds(0, RW)], in_sem.at[1]),
        pltpu.make_async_copy(wt_hbm, wsend.at[pl.ds(RW, RW)], in_sem.at[2]),
        pltpu.make_async_copy(wr_hbm, wsend.at[pl.ds(2 * RW, RW)], in_sem.at[3]),
        pltpu.make_async_copy(cot_hbm, cot_v, in_sem.at[4]),
    ]
    for load in loads:
        load.start()

    rep = (iota((RW, C), 1) % RW == iota((RW, C), 0)).astype(F32).astype(BF)
    here = (iota((8, C), 1) // RW == d)
    rows = [jnp.where(here, dot(jnp.broadcast_to(ref[...], (8, RW)), rep), 0.0)
            for ref in (att_ref, bias_ref, gain_ref, shift_ref)]
    line = iota((8, C), 0)
    placed = jnp.zeros((8, C), F32)
    for slot in range(4):
        placed = jnp.where(line == slot, rows[slot], placed)
    wsend[pl.ds(3 * RW, 16), :] = jnp.concatenate([placed, jnp.zeros((8, C), F32)], axis=0).astype(BF)

    def order(sign):
        j = iota((DEV, DEV), 0)
        k = j & 1
        a = (j >> 1) & (X - 1)
        b = (j // W8) & (Y - 1)
        c = j // (W8 * Y)
        dx, dy, dz = a, (a + b) & (Y - 1), (a + b + c) & (Z - 1)
        px = (mx + X + sign * dx) & (X - 1)
        py = (my + Y + sign * dy) & (Y - 1)
        pz = (mz + Z + sign * dz) & (Z - 1)
        dev = (px * 2 + ((mc + k) & 1)) * ND + py * Z + pz
        return (dev == iota((DEV, DEV), 1)).astype(F32).astype(BF)

    LB = 2 * CAP

    def list_of(slot, sign, tabs, mb):
        parts = jnp.concatenate([tabs[mb, 0] >> 5, tabs[mb, 0] & 31], axis=0)
        lists[slot] = dot_nt(order(sign), parts.astype(F32).astype(BF)).astype(BF)

    def expand(slot, i):
        e = iota((EC, DEV), 0) + i * EC
        pairs = ((e // CAP) == iota((EC, DEV), 1)).astype(F32).astype(BF)
        own = (iota((EC, LB), 0) & (CAP - 1)) == (iota((EC, LB), 1) & (CAP - 1))
        kept = jnp.where(own, dot(pairs, lists[slot]), 0.0).astype(BF)
        widen = jnp.where(iota((LB, 128), 0) < CAP, 32.0, 1.0).astype(BF)
        turn = jnp.where(iota((16, LB), 1) < CAP, 32.0, 1.0).astype(BF)
        return dot(kept, widen), dot_nt(turn, kept).astype(jnp.int32).astype(jnp.int16)

    def onehot_rows(col):
        wide = jnp.concatenate([col] * (N // 128), axis=1)
        return jnp.where(wide == iota(wide.shape, 1, jnp.int16), jnp.ones((), BF), jnp.zeros((), BF))

    def fill_turned(row, mb, dst):
        def step(i, carry):
            r = pl.multiple_of(i * 128, 128)
            ids = iota((128, EC), 0, jnp.int16) + (i * 128).astype(jnp.int16)
            for q in range(NCH):
                wide = jnp.concatenate([row[mb, q]] * 8, axis=0)
                dst[mb, pl.ds(r, 128), q * EC:(q + 1) * EC] = jnp.where(
                    wide == ids, jnp.ones((), BF), jnp.zeros((), BF)
                )
            return carry

        lax.fori_loop(0, N // 128, step, 0)

    def send_block(src, dst, mb, j, sign, ssem, rsem):
        rows = pl.ds(j * CAP, CAP)
        pltpu.make_async_remote_copy(
            src_ref=src.at[mb, rows], dst_ref=dst.at[mb, rows],
            send_sem=ssem.at[mb], recv_sem=rsem.at[mb, j // PER],
            device_id=place(j // W8, j % W8, sign), device_id_type=MESH,
        ).start()

    def send_chunk(src, dst, mb, i, sign, ssem, rsem):
        if i == 0:
            pltpu.make_async_copy(
                src.at[mb, pl.ds(0, CAP)], dst.at[mb, pl.ds(0, CAP)], rsem.at[mb, 0]
            ).start()
        for j in range(max(1, i * PER), (i + 1) * PER):
            send_block(src, dst, mb, j, sign, ssem, rsem)

    for mb in range(MB):
        list_of(mb, 1, esrc_ref, mb)
    loads[0].wait()
    pl.semaphore_wait(barrier, DEV - 1)

    def outgoing(mb, carry):
        for i in range(NCH):
            wide, flat = expand(mb, i)
            srow[mb, i] = flat
            hot = onehot_rows(wide.astype(jnp.int32).astype(jnp.int16))
            fs[mb, i * EC:(i + 1) * EC, :] = dot(hot, x_v[mb]).astype(BF)
            if i > 0:
                send_chunk(fs, fr, mb, i - 1, 1, fs_sem, fr_sem)
        send_chunk(fs, fr, mb, NCH - 1, 1, fs_sem, fr_sem)
        return carry

    for load in loads[1:4]:
        load.wait()
    half = pl.ds(pl.multiple_of(mc * HALF, 16), HALF)

    def send_weights(i, carry):
        pltpu.make_async_remote_copy(
            src_ref=wsend.at[half], dst_ref=wall.at[d, half],
            send_sem=w_sem.at[0], recv_sem=w_sem.at[1],
            device_id=(g, lax.rem(d + i, ND)), device_id_type=MESH,
        ).start()
        return carry

    lax.fori_loop(1, ND, send_weights, 0)
    pltpu.make_async_copy(wsend.at[half], wall.at[d, half], w_sem.at[1]).start()

    lax.fori_loop(0, MB, outgoing, 0)

    for mb in range(MB):
        list_of(MB + mb, -1, etgt_ref, mb)

    def incoming(mb, carry):
        for i in range(NCH):
            wide, flat = expand(MB + mb, i)
            rows = slice(i * EC, (i + 1) * EC)
            tcolf[mb, rows, :] = wide
            th[mb, rows, :] = onehot_rows(wide.astype(jnp.int32).astype(jnp.int16))
            trow[mb, i] = flat
        fill_turned(trow, mb, tht)
        return carry

    lax.fori_loop(0, MB, incoming, 0)
    for mb in range(MB):
        for i in range(N // 128):
            xt_v[mb, :, i * 128:(i + 1) * 128] = jnp.transpose(x_v[mb, i * 128:(i + 1) * 128, :])

    same = (iota((C, C), 0) // 64) == (iota((C, C), 1) // 64)
    eblk[...] = same.astype(F32).astype(BF)
    lane = iota((128, C), 0)
    head = iota((128, C), 1) // 64
    exp2[...] = ((lane < 8) & ((lane & 3) == head)).astype(F32).astype(BF)
    groups = N // 64
    r = lane & 63
    at = 2 * ((r & 31) // groups) + r // 32
    spread[...] = ((at == head) & ((r & 31) < 2 * groups)).astype(F32).astype(BF)
    pick = iota((C, 128), 0)
    slot = iota((C, 128), 1)
    sel[0] = ((pick == 64 * slot) & (slot < 4)).astype(F32).astype(BF)
    sel[1] = ((pick == 64 * (slot - 4)) & (slot >= 4) & (slot < 8)).astype(F32).astype(BF)
    vacc[...] = jnp.zeros_like(vacc)
    gacc[...] = jnp.zeros_like(gacc)

    mine = wall.at[:, half]
    pltpu.make_async_copy(mine, mine, w_sem.at[1]).wait()
    pltpu.make_async_remote_copy(
        src_ref=mine, dst_ref=mine, send_sem=w_sem.at[2], recv_sem=w_sem.at[3],
        device_id=twin, device_id_type=MESH,
    ).start()
    pltpu.make_async_copy(mine, mine, w_sem.at[3]).wait()
    for slot in range(3):
        wcat[:, slot * C:(slot + 1) * C] = wall[:, slot * RW:(slot + 1) * RW, :].reshape(C, C)
    vectors = jnp.sum(wall[:, 3 * RW:3 * RW + 16, :].astype(F32), axis=0)
    vecs[...] = vectors[0:8, :]
    att_col = jnp.transpose(jnp.broadcast_to(vecs[0:1, :], (C, C)))
    a2[...] = jnp.where(same, att_col, 0.0).astype(BF)

    def project(i, carry):
        mb, part = lax.div(i, N // NB), lax.rem(i, N // NB)
        rows = pl.ds(pl.multiple_of(part * NB, NB), NB)
        proj = dot(x_v[mb, rows, :], wcat[...])
        sp = proj[:, 0:C].astype(BF)
        tp = proj[:, C:2 * C]
        sp_v[mb, rows, :] = sp
        tp_v[mb, rows, :] = tp.astype(BF)
        rp_v[mb, rows, :] = proj[:, 2 * C:3 * C]
        gs, gp = gelu_pair(sp.astype(F32) + tp)
        hi, lo = split(gs)
        sg_v[mb, rows, :] = hi
        sga_v[mb, rows, :] = gp * vecs[0:1, :]
        ssc_v[mb, rows, :] = dot(hi, a2[...]) + dot(lo, a2[...])
        return carry

    lax.fori_loop(0, MB * (N // NB), project, 0)
    loads[4].wait()

    def fold(v):
        return jnp.sum(v.reshape(v.shape[0] // 8, 8, v.shape[1]), axis=0)

    def edge_rows(i):
        return slice(i * EC, (i + 1) * EC)

    def score_chunk(mb, i):
        rows = edge_rows(i)
        part = fr.at[mb, pl.ds(i * EC, EC)]
        pltpu.make_async_copy(part, part, fr_sem.at[mb, i]).wait()
        se = dot(fr[mb, rows, :], wcat[:, 0:C]).astype(BF)
        se_v[rows, :] = se
        z = se.astype(F32) + dot(th[mb, rows, :], tp_v[mb])
        ge, gp = gelu_pair(z)
        hi, lo = split(ge)
        g_v[rows, :] = hi
        ga_v[rows, :] = gp * vecs[0:1, :]
        sc_v[rows, :] = dot(hi, a2[...]) + dot(lo, a2[...])

    def sweep_chunk(mb, i):
        low = (iota((128, 128), 1) & 63).astype(F32)
        for q in range(EC // 128):
            part = slice(i * EC + q * 128, i * EC + (q + 1) * 128)
            tgt = tcolf[mb, part, :]
            s0, s1 = sc_v[part, 0:128], sc_v[part, 128:256]
            for grp in range(groups):
                hit = tgt == low + (64.0 * grp)
                for side, s in enumerate((s0, s1)):
                    top = jnp.max(jnp.where(hit, s, LOWEST).reshape(16, 8, 128), axis=0)
                    at = side * groups + grp
                    mx_v[at] = jnp.maximum(mx_v[at], top)

    def forward_edges(mb):
        mx_v[...] = jnp.full(mx_v.shape, LOWEST, F32)
        for i in range(NCH):
            score_chunk(mb, i)
            if i > 0:
                sweep_chunk(mb, i - 1)
        sweep_chunk(mb, NCH - 1)

    def tops(mb):
        tall = [mx_v[at] for at in range(2 * groups)]
        for shift in (4, 2, 1):
            tall = [jnp.maximum(v, pltpu.roll(v, shift, 0)) for v in tall]
        sub = iota((8, 128), 0)
        best = []
        for at in range(0, 2 * groups, 8):
            row = tall[at]
            for k in range(1, min(8, 2 * groups - at)):
                row = jnp.where(sub == k, tall[at + k], row)
            best.append(row)
        best = jnp.concatenate(best + [jnp.zeros((128 - 8 * len(best), 128), F32)], axis=0)
        turned = jnp.transpose(best)
        both = turned[0:64, :] + pltpu.roll(turned[64:128, :], 32, 1)
        hi = both.astype(BF).astype(F32)
        table = hi + pltpu.roll(both - hi, 64, 1)
        for i in range(N // NB):
            rows = slice(i * NB, (i + 1) * NB)
            whose = iota((NB, 128), 0) // 64 + i * (NB // 64)
            mine = jnp.concatenate([table] * (NB // 64), axis=0)
            mine = jnp.where((iota((NB, 128), 1) & (groups - 1)) == whose, mine, 0.0).astype(BF)
            own = ssc_v[mb, rows, :]
            hi, lo = split(jnp.maximum(dot(mine, spread[...]), own))
            ssc_v[mb, rows, :] = jnp.exp(own - (hi.astype(F32) + lo.astype(F32)))
            mtab[rows, :] = (dot(hi, sel[0]) + dot(lo, sel[1])).astype(BF)

    def weigh(mb):
        for i in range(NCH):
            rows = edge_rows(i)
            me = dot(th[mb, rows, :], mtab[...]).astype(BF)
            live = tcolf[mb, rows, :] >= 0.0
            live = jnp.concatenate([live, live], axis=1)
            p = jnp.where(live, jnp.exp(sc_v[rows, :] - dot(me, exp2[...])), 0.0)
            pv_v[rows, 0:C] = (p * se_v[rows, :].astype(F32)).astype(BF)
            pv_v[rows, C:2 * C] = p.astype(BF)

    def nodes(mb):
        for i in range(N // NB):
            rows = slice(i * NB, (i + 1) * NB)
            sc_v[rows, :] = dot(tht[mb, rows, :], pv_v[:, 0:C])
            sc_v[N + i * NB:N + (i + 1) * NB, :] = dot(tht[mb, rows, :], pv_v[:, C:2 * C])
        for i in range(N // NB):
            r = i * NB
            rows = slice(r, r + NB)
            ps = ssc_v[mb, rows, :]
            inv = 1.0 / (sc_v[N + r:N + r + NB, :] + ps)
            sp = sp_v[mb, rows, :].astype(F32)
            agg = (sc_v[rows, :] + ps * sp) * inv
            alpha = ps * inv
            live = (iota((NB, 1), 0) + r < cnt_ref[0, mb]).astype(F32)
            pre = agg + vecs[1:2, :] + rp_v[mb, rows, :]
            centre = pre - jnp.mean(pre, axis=1, keepdims=True)
            rstd = lax.rsqrt(jnp.mean(centre * centre, axis=1, keepdims=True) + 1e-05)
            nrm = centre * rstd
            lin = nrm * vecs[2:3, :] + vecs[3:4, :]
            e = jnp.exp(jnp.minimum(lin, 0.0))
            up = lin > 0
            x_v2 = jnp.where(up, lin, e - 1.0) * live
            cot = cot_v[mb, rows, :].astype(F32) * live
            cot_v[mb, rows, :] = x_v2.astype(BF)
            dlin = cot * jnp.where(up, 1.0, e)
            vacc[2] += fold(dlin * nrm)
            vacc[3] += fold(dlin)
            dn = dlin * vecs[2:3, :]
            dpre = rstd * (
                dn
                - jnp.mean(dn, axis=1, keepdims=True)
                - nrm * jnp.mean(dn * nrm, axis=1, keepdims=True)
            )
            vacc[1] += fold(dpre)
            loc_v[mb, rows, 2 * C:3 * C] = dpre.astype(BF)
            dagr = (dpre * inv).astype(BF)
            dagf = dagr.astype(F32)
            hi, lo = split(dagf * agg)
            big = dot(hi, eblk[...]) + dot(lo, eblk[...])
            hi, lo = split(dagf * (sp - agg))
            ds = ps * (dot(hi, eblk[...]) + dot(lo, eblk[...]))
            vacc[0] += fold(ds * sg_v[mb, rows, :].astype(F32))
            dz = ds * sga_v[mb, rows, :].astype(F32)
            loc_v[mb, rows, C:2 * C] = dz.astype(BF)
            loc_v[mb, rows, 0:C] = (alpha * dpre + dz).astype(BF)
            dtab[rows, 0:C] = dagr
            hi, lo = split(big)
            dtab[rows, C:C + 128] = (dot(hi, sel[0]) + dot(lo, sel[1])).astype(BF)

    def grad_chunk(mb, i):
        rows = edge_rows(i)
        got = dot(th[mb, rows, :], dtab[...])
        dag = got[:, 0:C]
        se = se_v[rows, :].astype(F32)
        hi, lo = split(dag * se)
        p = pv_v[rows, C:2 * C].astype(F32)
        ds = p * (dot(hi, eblk[...]) + dot(lo, eblk[...]) - dot(got[:, C:C + 128].astype(BF), exp2[...]))
        vacc[0] += fold(ds * g_v[rows, :].astype(F32))
        dz = ds * ga_v[rows, :]
        eg = (p * dag + dz).astype(BF)
        rs[mb, rows, :] = eg
        fs[mb, rows, :] = dz.astype(BF)

    def backward_edges(mb):
        for i in range(NCH):
            grad_chunk(mb, i)
            if i > 0:
                send_chunk(rs, rr, mb, i - 1, -1, rs_sem, rr_sem)
        send_chunk(rs, rr, mb, NCH - 1, -1, rs_sem, rr_sem)

    most = pl.ds(0, (DEV - 1) * CAP)

    def one_batch(mb, carry):
        forward_edges(mb)
        tops(mb)
        weigh(mb)
        nodes(mb)
        pltpu.make_async_copy(cot_v.at[mb], out_hbm.at[mb], out_sem.at[mb]).start()
        pltpu.make_async_copy(fs.at[mb, most], fs.at[mb, most], fs_sem.at[mb]).wait()
        backward_edges(mb)
        return carry

    lax.fori_loop(0, MB, one_batch, 0)

    def local_grads(mb, carry):
        for i in range(N // NB):
            rows = slice(i * NB, (i + 1) * NB)
            dtgt = dot(tht[mb, rows, :], fs[mb]) + loc_v[mb, rows, C:2 * C].astype(F32)
            loc_v[mb, rows, C:2 * C] = dtgt.astype(BF)
        gacc[...] += dot(xt_v[mb], loc_v[mb])
        gacc[:, 0:C] += dot_tn(fr[mb], rs[mb])
        return carry

    lax.fori_loop(0, MB, local_grads, 0)

    def pack_vectors(v):
        hi = v.astype(BF).astype(F32)
        return jnp.concatenate([hi, v - hi], axis=0).astype(BF)

    def repack(v):
        cut = HALF - 16
        both = v[..., cut:cut + 8, :] + v[..., cut + 8:cut + 16, :]
        hi = both.astype(BF).astype(F32)
        last = jnp.concatenate([hi, both - hi], axis=-2)
        last = jnp.where(mc == 1, last, v[..., cut:cut + 16, :])
        return jnp.concatenate([v[..., 0:cut, :], last], axis=-2).astype(BF)

    for slot in range(3):
        g0s[:, slot * RW:(slot + 1) * RW, :] = gacc[:, slot * C:(slot + 1) * C].astype(BF).reshape(ND, RW, C)
    sums = [jnp.sum(vacc[slot], axis=0, keepdims=True) for slot in range(4)]
    packed = pack_vectors(jnp.concatenate(sums + [jnp.zeros((4, C), F32)], axis=0))
    for slot in range(ND):
        g0s[slot, 3 * RW:3 * RW + 16, :] = packed
    other = pl.ds(pl.multiple_of((1 - mc) * HALF, 16), HALF)
    pltpu.make_async_remote_copy(
        src_ref=g0s.at[:, other], dst_ref=g0r, send_sem=r_sem.at[4], recv_sem=r_sem.at[5],
        device_id=twin, device_id_type=MESH,
    ).start()

    def partials(mb, carry):
        for i in range(N // NB):
            rows = slice(i * NB, (i + 1) * NB)
            rp_v[mb, rows, :] = dot_nt(loc_v[mb, rows, C:3 * C], wcat[:, C:3 * C])
        fill_turned(srow, mb, tht)
        return carry

    partials(0, 0)
    pltpu.make_async_copy(g0r, g0r, r_sem.at[5]).wait()
    g1s[...] = repack(g0s[:, half, :].astype(F32) + g0r[...].astype(F32))

    def send_first(i, carry):
        to = lax.rem(d + i, ND)
        pltpu.make_async_remote_copy(
            src_ref=g1s.at[to], dst_ref=g1r.at[d], send_sem=r_sem.at[0], recv_sem=r_sem.at[1],
            device_id=(g, to), device_id_type=MESH,
        ).start()
        return carry

    lax.fori_loop(1, ND, send_first, 0)
    pltpu.make_async_copy(g1s.at[d], g1r.at[d], r_sem.at[1]).start()
    partials(1, 0)

    def finish(mb):
        for i in range(NCH):
            rows = pl.ds(i * EC, EC)
            pltpu.make_async_copy(rr.at[mb, rows], rr.at[mb, rows], rr_sem.at[mb, i]).wait()
        pltpu.make_async_copy(cot_v.at[mb], out_hbm.at[mb], out_sem.at[mb]).wait()

        def step(i, carry):
            rows = pl.ds(pl.multiple_of(i * NB, NB), NB)
            dsrc = (dot(tht[mb, rows, :], rr[mb]) + loc_v[mb, rows, 0:C].astype(F32)).astype(BF)
            cot_v[mb, rows, :] = (dot_nt(dsrc, wcat[:, 0:C]) + rp_v[mb, rows, :]).astype(BF)
            return carry

        lax.fori_loop(0, N // NB, step, 0)
        pltpu.make_async_copy(cot_v.at[mb], gf_hbm.at[mb], out_sem.at[mb]).start()

    finish(0)

    pltpu.make_async_copy(g1r, g1r, r_sem.at[1]).wait()
    g2s[...] = repack(jnp.sum(g1r[...].astype(F32), axis=0))

    def send_second(i, carry):
        pltpu.make_async_remote_copy(
            src_ref=g2s, dst_ref=g2r.at[g], send_sem=r_sem.at[2], recv_sem=r_sem.at[3],
            device_id=(lax.rem(g + i, NG), d), device_id_type=MESH,
        ).start()
        return carry

    lax.fori_loop(1, NG, send_second, 0)
    pltpu.make_async_copy(g2s, g2r.at[g], r_sem.at[3]).start()

    for mb in range(1, MB):
        finish(mb)

    pltpu.make_async_copy(g2r, g2r, r_sem.at[3]).wait()
    for side in range(2):
        total = g2r[side].astype(F32)
        for slot in range(1, X):
            total = total + g2r[2 * slot + side].astype(F32)
        small_ref[side * HALF:(side + 1) * HALF, :] = total
    tail = small_ref[3 * RW:3 * RW + 8, :] + small_ref[3 * RW + 8:3 * RW + 16, :]
    small_ref[3 * RW:3 * RW + 8, :] = pltpu.roll(tail, lax.rem(C - d * RW, C), 1)

    for mb in range(MB):
        pltpu.make_async_copy(cot_v.at[mb], gf_hbm.at[mb], out_sem.at[mb]).wait()
        pltpu.make_async_copy(rs.at[mb, most], rs.at[mb, most], rs_sem.at[mb]).wait()
    pltpu.make_async_copy(mine, mine, w_sem.at[2]).wait()
    others = pl.ds(0, ND - 1)
    mine = wall.at[others, half]
    pltpu.make_async_copy(mine, mine, w_sem.at[0]).wait()
    pltpu.make_async_copy(g0r, g0r, r_sem.at[4]).wait()
    pltpu.make_async_copy(g1s.at[others], g1s.at[others], r_sem.at[0]).wait()
    others = pl.ds(0, NG - 1)
    pltpu.make_async_copy(g2r.at[others], g2r.at[others], r_sem.at[2]).wait()


def hand_on(RW, out_in, gf_in, small_in, out_hbm, gf_hbm, gws, gwt, gwr, v0, v1, v2, v3, held, sems):
    MB = out_in.shape[0]
    loads, stores = [], []
    for mb in range(MB):
        for src, dst in ((out_in, out_hbm), (gf_in, gf_hbm)):
            slot = len(loads)
            loads.append(pltpu.make_async_copy(src.at[mb], held.at[slot], sems.at[0, slot]))
            stores.append(pltpu.make_async_copy(held.at[slot], dst.at[mb], sems.at[1, slot]))
    for load in loads:
        load.start()
    for slot, dst in enumerate((gws, gwt, gwr)):
        dst[...] = small_in[slot * RW:(slot + 1) * RW, :]
    for slot, dst in enumerate((v0, v1, v2, v3)):
        dst[...] = small_in[3 * RW + slot:3 * RW + slot + 1, 0:RW]
    for load, store in zip(loads, stores):
        load.wait()
        store.start()
    for store in stores:
        store.wait()


def local(
    shape,
    features, w_source, w_target, w_residual, attention, out_bias, norm_gain, norm_shift,
    node_count, edge_src, edge_tgt, cotangent,
):
    NG, ND = shape
    X = NG // 2
    Y = 1
    while Y * Y < ND:
        Y *= 2
    Z = ND // Y
    MB, N, C = features.shape
    CAP = edge_src.shape[3]
    DEV = NG * ND
    E = DEV * CAP
    EC = min(256, E // 2)
    NCH = E // EC
    RW = C // ND
    PK = 3 * RW + 16
    groups = N // 64
    vmem = pl.BlockSpec(memory_space=pltpu.VMEM)
    hbm = pl.BlockSpec(memory_space=pl.ANY)
    smem = pl.BlockSpec(memory_space=pltpu.SMEM)
    cfg = (NG, ND, X, Y, Z, N, CAP, MB, EC)
    V = pltpu.VMEM
    DMA = pltpu.SemaphoreType.DMA
    I16 = jnp.int16
    wide = jax.ShapeDtypeStruct((MB, N, C), BF)
    block = jax.ShapeDtypeStruct((RW, C), F32)
    line = jax.ShapeDtypeStruct((1, RW), F32)
    result, grad_rows, small = pl.pallas_call(
        functools.partial(kernel, cfg),
        out_shape=(wide, wide, jax.ShapeDtypeStruct((PK, C), F32)),
        in_specs=[smem] + [vmem] * 6 + [hbm] * 5,
        out_specs=(hbm, hbm, vmem),
        scratch_shapes=[
            V((MB, N, C), BF), V((MB, C, N), BF), V((MB, N, C), BF),
            V((MB, E, C), BF), V((MB, E, C), BF), V((MB, E, C), BF), V((MB, E, C), BF),
            V((PK, C), BF), V((ND, PK, C), BF), V((C, 3 * C), BF),
            V((2 * MB, DEV, 2 * CAP), BF), V((MB, E, 128), F32),
            V((MB, NCH, 16, EC), I16), V((MB, NCH, 16, EC), I16),
            V((MB, E, N), BF), V((MB, N, E), BF),
            V((E, C), BF), V((E, C), BF), V((E, C), F32), V((max(E, 2 * N), C), F32), V((E, 2 * C), BF),
            V((MB, N, C), BF), V((MB, N, C), BF), V((MB, N, C), F32),
            V((MB, N, C), BF), V((MB, N, C), F32), V((MB, N, C), F32),
            V((N, 128), BF), V((2 * groups, 8, 128), F32),
            V((N, C + 128), BF), V((MB, N, 3 * C), BF),
            V((C, C), BF), V((C, C), BF), V((128, C), BF), V((128, C), BF), V((2, C, 128), BF),
            V((8, C), F32), V((4, 8, C), F32), V((C, 3 * C), F32),
            V((ND, PK, C), BF), V((ND, PK // 2, C), BF), V((ND, PK // 2, C), BF),
            V((ND, PK // 2, C), BF), V((PK // 2, C), BF), V((NG, PK // 2, C), BF),
            DMA((5,)), DMA((MB,)), DMA((MB, NCH)), DMA((MB,)), DMA((MB, NCH)),
            DMA((4,)), DMA((6,)), DMA((MB,)),
        ],
        compiler_params=pltpu.CompilerParams(
            collective_id=0, has_side_effects=True, vmem_limit_bytes=62 * 2**20
        ),
        cost_estimate=pl.CostEstimate(
            flops=20 * MB * E * N * C, bytes_accessed=10 * MB * N * C, transcendentals=4 * MB * E * C
        ),
    )(
        jnp.swapaxes(node_count, 0, 1), jnp.swapaxes(edge_src, 2, 3), jnp.swapaxes(edge_tgt, 2, 3),
        attention.reshape(1, RW), out_bias.reshape(1, RW), norm_gain.reshape(1, RW), norm_shift.reshape(1, RW),
        features, cotangent, w_source, w_target, w_residual,
    )
    outs = pl.pallas_call(
        functools.partial(hand_on, RW),
        out_shape=(wide, wide, block, block, block, line, line, line, line),
        in_specs=[hbm, hbm, vmem],
        out_specs=(hbm, hbm) + (vmem,) * 7,
        scratch_shapes=[V((2 * MB, N, C), BF), DMA((2, 2 * MB))],
    )(result, grad_rows, small)
    return outs[:5] + tuple(v.reshape(RW) for v in outs[5:])


def solution(mesh):
    shape = (mesh.shape["grp"], mesh.shape["dev"])
    return jax.shard_map(
        functools.partial(local, shape),
        mesh=mesh,
        in_specs=(
            P(None, ("grp", "dev"), None),
            P("dev", None),
            P("dev", None),
            P("dev", None),
            P("dev"),
            P("dev"),
            P("dev"),
            P("dev"),
            P(None, ("grp", "dev")),
            P(None, ("grp", "dev"), None, None),
            P(None, ("grp", "dev"), None, None),
            P(None, ("grp", "dev"), None),
        ),
        out_specs=(
            P(None, ("grp", "dev"), None),
            P(None, ("grp", "dev"), None),
            P("dev", None),
            P("dev", None),
            P("dev", None),
            P("dev"),
            P("dev"),
            P("dev"),
            P("dev"),
        ),
        check_vma=False,
    )
```

```python
import functools

import jax
import jax.numpy as jnp
from jax import lax
from jax.experimental import pallas as pl
from jax.experimental.pallas import tpu as pltpu
from jax.sharding import PartitionSpec as P

MESH = pl.DeviceIdType.MESH
BF = jnp.bfloat16
F32 = jnp.float32
H = 4
LOWEST = -1e30
C0 = 0.7978845608028654
C1 = 0.044715


def dot(a, b):
    return jnp.dot(a, b, preferred_element_type=F32)


def dot_nt(a, b):
    return lax.dot_general(a, b, (((1,), (1,)), ((), ())), preferred_element_type=F32)


def dot_tn(a, b):
    return lax.dot_general(a, b, (((0,), (0,)), ((), ())), preferred_element_type=F32)


def iota(shape, axis, kind=jnp.int32):
    return lax.broadcasted_iota(kind, shape, axis)


def gelu_pair(z):
    zz = z * z
    t = jnp.tanh(z * (C0 + (C0 * C1) * zz))
    half = 0.5 * z
    g = half + half * t
    gp = (0.5 + 0.5 * t) + (half - half * (t * t)) * (C0 + (3.0 * C0 * C1) * zz)
    return g, gp


def split(v):
    hi = v.astype(BF)
    return hi, (v - hi.astype(F32)).astype(BF)


def kernel(
    cfg,
    cnt_ref, esrc_ref, etgt_ref, att_ref, bias_ref, gain_ref, shift_ref,
    x_hbm, cot_hbm, ws_hbm, wt_hbm, wr_hbm,
    out_hbm, gf_hbm, small_ref,
    x_v, cot_v, fs, fr, rs, rr, wsend, wall, wcat,
    lists, tcolf, trow, srow, th, tht,
    se_v, g_v, ga_v, sc_v, pv_v, sp_v, tp_v, rp_v, sg_v, sga_v, ssc_v, mtab, mx_v,
    dtab, loc_v, a2, eblk, exp2, spread, sel, vecs, vacc, gacc,
    g0s, g0r, g1s, g1r, g2s, g2r,
    in_sem, fs_sem, fr_sem, rs_sem, rr_sem, w_sem, r_sem, out_sem,
):
    NG, ND, X, Y, Z, N, CAP, MB, EC = cfg
    C = 256
    DEV = NG * ND
    E = DEV * CAP
    NCH = E // EC
    PER = EC // CAP
    RW = C // ND
    PK = 3 * RW + 16
    HALF = PK // 2
    NB = min(256, N)
    W8 = 2 * X
    STEP = 1
    g, d = lax.axis_index("grp"), lax.axis_index("dev")
    mx, mc = lax.div(g, 2), lax.rem(g, 2)
    my, mz = lax.div(d, Z), lax.rem(d, Z)
    twin = (mx * 2 + 1 - mc, d)

    def place(i, q, sign):
        a, k = q // 2, q % 2
        if isinstance(i, int):
            b, c = i % Y, i // Y
            dy, dz = (a + b) % Y, (a + b + c) % Z
        else:
            b, c = lax.rem(i, Y), lax.div(i, Y)
            dy, dz = lax.rem(a + b, Y), lax.rem(a + b + c, Z)
        if sign > 0:
            px, py, pz = mx + a, my + dy, mz + dz
        else:
            px, py, pz = mx + (X - a), my + (Y - dy), mz + (Z - dz)
        return (
            lax.rem(px, X) * 2 + lax.rem(mc + k, 2),
            lax.rem(py, Y) * Z + lax.rem(pz, Z),
        )

    loads = [
        pltpu.make_async_copy(x_hbm, x_v, in_sem.at[0]),
        pltpu.make_async_copy(ws_hbm, wsend.at[pl.ds(0, RW)], in_sem.at[1]),
        pltpu.make_async_copy(wt_hbm, wsend.at[pl.ds(RW, RW)], in_sem.at[2]),
        pltpu.make_async_copy(wr_hbm, wsend.at[pl.ds(2 * RW, RW)], in_sem.at[3]),
        pltpu.make_async_copy(cot_hbm, cot_v, in_sem.at[4]),
    ]
    for load in loads:
        load.start()

    barrier = pltpu.get_barrier_semaphore()

    def greet(i, q):
        pl.semaphore_signal(barrier, inc=1, device_id=place(i, q, 1), device_id_type=MESH)

    for j in range(1, DEV):
        greet(j // W8, j % W8)
    rep = (iota((RW, C), 1) % RW == iota((RW, C), 0)).astype(F32).astype(BF)
    here = (iota((8, C), 1) // RW == d)
    rows = [jnp.where(here, dot(jnp.broadcast_to(ref[...], (8, RW)), rep), 0.0)
            for ref in (att_ref, bias_ref, gain_ref, shift_ref)]
    line = iota((8, C), 0)
    placed = jnp.zeros((8, C), F32)
    for slot in range(4):
        placed = jnp.where(line == slot, rows[slot], placed)
    wsend[pl.ds(3 * RW, 16), :] = jnp.concatenate([placed, jnp.zeros((8, C), F32)], axis=0).astype(BF)

    def order(sign):
        j = iota((DEV, DEV), 0)
        k = j & 1
        a = (j >> 1) & (X - 1)
        b = (j // W8) & (Y - 1)
        c = j // (W8 * Y)
        dx, dy, dz = a, (a + b) & (Y - 1), (a + b + c) & (Z - 1)
        px = (mx + X + sign * dx) & (X - 1)
        py = (my + Y + sign * dy) & (Y - 1)
        pz = (mz + Z + sign * dz) & (Z - 1)
        dev = (px * 2 + ((mc + k) & 1)) * ND + py * Z + pz
        return (dev == iota((DEV, DEV), 1)).astype(F32).astype(BF)

    LB = 2 * CAP

    def list_of(slot, sign, tabs, mb):
        parts = jnp.concatenate([tabs[mb, 0] >> 5, tabs[mb, 0] & 31], axis=0)
        lists[slot] = dot_nt(order(sign), parts.astype(F32).astype(BF)).astype(BF)

    def expand(slot, i):
        e = iota((EC, DEV), 0) + i * EC
        pairs = ((e // CAP) == iota((EC, DEV), 1)).astype(F32).astype(BF)
        own = (iota((EC, LB), 0) & (CAP - 1)) == (iota((EC, LB), 1) & (CAP - 1))
        kept = jnp.where(own, dot(pairs, lists[slot]), 0.0).astype(BF)
        widen = jnp.where(iota((LB, 128), 0) < CAP, 32.0, 1.0).astype(BF)
        turn = jnp.where(iota((16, LB), 1) < CAP, 32.0, 1.0).astype(BF)
        return dot(kept, widen), dot_nt(turn, kept).astype(jnp.int32).astype(jnp.int16)

    def onehot_rows(col):
        wide = jnp.concatenate([col] * (N // 128), axis=1)
        return jnp.where(wide == iota(wide.shape, 1, jnp.int16), jnp.ones((), BF), jnp.zeros((), BF))

    def fill_turned(row, mb, dst):
        def step(i, carry):
            r = pl.multiple_of(i * 128, 128)
            ids = iota((128, EC), 0, jnp.int16) + (i * 128).astype(jnp.int16)
            for q in range(NCH):
                wide = jnp.concatenate([row[mb, q]] * 8, axis=0)
                dst[mb, pl.ds(r, 128), q * EC:(q + 1) * EC] = jnp.where(
                    wide == ids, jnp.ones((), BF), jnp.zeros((), BF)
                )
            return carry

        lax.fori_loop(0, N // 128, step, 0)

    def send_block(src, dst, mb, j, sign, ssem, rsem):
        rows = pl.ds(j * CAP, CAP)
        pltpu.make_async_remote_copy(
            src_ref=src.at[mb, rows], dst_ref=dst.at[mb, rows],
            send_sem=ssem.at[mb], recv_sem=rsem.at[mb, j // PER],
            device_id=place(j // W8, j % W8, sign), device_id_type=MESH,
        ).start()

    def send_chunk(src, dst, mb, i, sign, ssem, rsem):
        if i == 0:
            pltpu.make_async_copy(
                src.at[mb, pl.ds(0, CAP)], dst.at[mb, pl.ds(0, CAP)], rsem.at[mb, 0]
            ).start()
        for j in range(max(1, i * PER), (i + 1) * PER):
            send_block(src, dst, mb, j, sign, ssem, rsem)

    for mb in range(MB):
        list_of(mb, 1, esrc_ref, mb)
    loads[0].wait()
    pl.semaphore_wait(barrier, DEV - 1)

    def outgoing(mb, carry):
        for i in range(NCH):
            wide, flat = expand(mb, i)
            srow[mb, i] = flat
            hot = onehot_rows(wide.astype(jnp.int32).astype(jnp.int16))
            fs[mb, i * EC:(i + 1) * EC, :] = dot(hot, x_v[mb]).astype(BF)
            if i > 0:
                send_chunk(fs, fr, mb, i - 1, 1, fs_sem, fr_sem)
        send_chunk(fs, fr, mb, NCH - 1, 1, fs_sem, fr_sem)
        return carry

    for load in loads[1:4]:
        load.wait()
    half = pl.ds(pl.multiple_of(mc * HALF, 16), HALF)

    def send_weights(i, carry):
        pltpu.make_async_remote_copy(
            src_ref=wsend.at[half], dst_ref=wall.at[d, half],
            send_sem=w_sem.at[0], recv_sem=w_sem.at[1],
            device_id=(g, lax.rem(d + i, ND)), device_id_type=MESH,
        ).start()
        return carry

    lax.fori_loop(1, ND, send_weights, 0)
    pltpu.make_async_copy(wsend.at[half], wall.at[d, half], w_sem.at[1]).start()

    lax.fori_loop(0, MB, outgoing, 0)

    for mb in range(MB):
        list_of(MB + mb, -1, etgt_ref, mb)

    def incoming(mb, carry):
        for i in range(NCH):
            wide, flat = expand(MB + mb, i)
            rows = slice(i * EC, (i + 1) * EC)
            tcolf[mb, rows, :] = wide
            th[mb, rows, :] = onehot_rows(wide.astype(jnp.int32).astype(jnp.int16))
            trow[mb, i] = flat
        fill_turned(trow, mb, tht)
        return carry

    lax.fori_loop(0, MB, incoming, 0)
    same = (iota((C, C), 0) // 64) == (iota((C, C), 1) // 64)
    eblk[...] = same.astype(F32).astype(BF)
    lane = iota((128, C), 0)
    head = iota((128, C), 1) // 64
    exp2[...] = ((lane < 8) & ((lane & 3) == head)).astype(F32).astype(BF)
    groups = N // 64
    r = lane & 63
    at = 2 * ((r & 31) // groups) + r // 32
    spread[...] = ((at == head) & ((r & 31) < 2 * groups)).astype(F32).astype(BF)
    pick = iota((C, 128), 0)
    slot = iota((C, 128), 1)
    sel[0] = ((pick == 64 * slot) & (slot < 4)).astype(F32).astype(BF)
    sel[1] = ((pick == 64 * (slot - 4)) & (slot >= 4) & (slot < 8)).astype(F32).astype(BF)
    vacc[...] = jnp.zeros_like(vacc)
    gacc[...] = jnp.zeros_like(gacc)

    mine = wall.at[:, half]
    pltpu.make_async_copy(mine, mine, w_sem.at[1]).wait()
    pltpu.make_async_remote_copy(
        src_ref=mine, dst_ref=mine, send_sem=w_sem.at[2], recv_sem=w_sem.at[3],
        device_id=twin, device_id_type=MESH,
    ).start()
    pltpu.make_async_copy(mine, mine, w_sem.at[3]).wait()
    for slot in range(3):
        wcat[:, slot * C:(slot + 1) * C] = wall[:, slot * RW:(slot + 1) * RW, :].reshape(C, C)
    vectors = jnp.sum(wall[:, 3 * RW:3 * RW + 16, :].astype(F32), axis=0)
    vecs[...] = vectors[0:8, :]
    att_col = jnp.transpose(jnp.broadcast_to(vecs[0:1, :], (C, C)))
    a2[...] = jnp.where(same, att_col, 0.0).astype(BF)

    def project(i, carry):
        mb, part = lax.div(i, N // NB), lax.rem(i, N // NB)
        rows = pl.ds(pl.multiple_of(part * NB, NB), NB)
        proj = dot(x_v[mb, rows, :], wcat[...])
        sp = proj[:, 0:C].astype(BF)
        tp = proj[:, C:2 * C]
        sp_v[mb, rows, :] = sp
        tp_v[mb, rows, :] = tp.astype(BF)
        rp_v[mb, rows, :] = proj[:, 2 * C:3 * C]
        gs, gp = gelu_pair(sp.astype(F32) + tp)
        hi, lo = split(gs)
        sg_v[mb, rows, :] = hi
        sga_v[mb, rows, :] = gp * vecs[0:1, :]
        ssc_v[mb, rows, :] = dot(hi, a2[...]) + dot(lo, a2[...])
        return carry

    lax.fori_loop(0, MB * (N // NB), project, 0)
    loads[4].wait()

    def fold(v):
        return jnp.sum(v.reshape(v.shape[0] // 8, 8, v.shape[1]), axis=0)

    def edge_rows(i):
        return slice(i * EC, (i + 1) * EC)

    def score_chunk(mb, i):
        rows = edge_rows(i)
        se = dot(fr[mb, rows, :], wcat[:, 0:C]).astype(BF)
        se_v[rows, :] = se
        z = se.astype(F32) + dot(th[mb, rows, :], tp_v[mb])
        ge, gp = gelu_pair(z)
        hi, lo = split(ge)
        g_v[rows, :] = hi
        ga_v[rows, :] = gp * vecs[0:1, :]
        sc_v[rows, :] = dot(hi, a2[...]) + dot(lo, a2[...])

    def sweep_chunk(mb, i):
        low = (iota((64, 128), 1) & 63).astype(F32)
        for q in range(EC // 64):
            part = slice(i * EC + q * 64, i * EC + (q + 1) * 64)
            tgt = tcolf[mb, part, :]
            s0, s1 = sc_v[part, 0:128], sc_v[part, 128:256]
            for grp in range(groups):
                hit = tgt == low + (64.0 * grp)
                for side, s in enumerate((s0, s1)):
                    top = jnp.max(jnp.where(hit, s, LOWEST).reshape(8, 8, 128), axis=0)
                    at = side * groups + grp
                    mx_v[at] = jnp.maximum(mx_v[at], top)

    def forward_edges(mb):
        mx_v[...] = jnp.full(mx_v.shape, LOWEST, F32)
        for i in range(NCH):
            if i % STEP == 0:
                for k in range(i, min(i + STEP, NCH)):
                    part = fr.at[mb, pl.ds(k * EC, EC)]
                    pltpu.make_async_copy(part, part, fr_sem.at[mb, k]).wait()
            score_chunk(mb, i)
            if i > 0:
                sweep_chunk(mb, i - 1)
        sweep_chunk(mb, NCH - 1)

    def tops(mb):
        tall = [mx_v[at] for at in range(2 * groups)]
        for shift in (4, 2, 1):
            tall = [jnp.maximum(v, pltpu.roll(v, shift, 0)) for v in tall]
        sub = iota((8, 128), 0)
        best = []
        for at in range(0, 2 * groups, 8):
            row = tall[at]
            for k in range(1, min(8, 2 * groups - at)):
                row = jnp.where(sub == k, tall[at + k], row)
            best.append(row)
        best = jnp.concatenate(best + [jnp.zeros((128 - 8 * len(best), 128), F32)], axis=0)
        turned = jnp.transpose(best)
        both = turned[0:64, :] + pltpu.roll(turned[64:128, :], 32, 1)
        hi = both.astype(BF).astype(F32)
        table = hi + pltpu.roll(both - hi, 64, 1)
        for i in range(N // NB):
            rows = slice(i * NB, (i + 1) * NB)
            whose = iota((NB, 128), 0) // 64 + i * (NB // 64)
            mine = jnp.concatenate([table] * (NB // 64), axis=0)
            mine = jnp.where((iota((NB, 128), 1) & (groups - 1)) == whose, mine, 0.0).astype(BF)
            own = ssc_v[mb, rows, :]
            hi, lo = split(jnp.maximum(dot(mine, spread[...]), own))
            ssc_v[mb, rows, :] = jnp.exp(own - (hi.astype(F32) + lo.astype(F32)))
            mtab[rows, :] = (dot(hi, sel[0]) + dot(lo, sel[1])).astype(BF)

    def weigh(mb):
        for i in range(NCH):
            rows = edge_rows(i)
            me = dot(th[mb, rows, :], mtab[...]).astype(BF)
            live = tcolf[mb, rows, :] >= 0.0
            live = jnp.concatenate([live, live], axis=1)
            p = jnp.where(live, jnp.exp(sc_v[rows, :] - dot(me, exp2[...])), 0.0)
            rs[mb, rows, :] = (p * se_v[rows, :].astype(F32)).astype(BF)
            pv_v[rows, :] = p.astype(BF)

    def nodes(mb):
        for i in range(N // NB):
            rows = slice(i * NB, (i + 1) * NB)
            sc_v[rows, :] = dot(tht[mb, rows, :], rs[mb])
            sc_v[N + i * NB:N + (i + 1) * NB, :] = dot(tht[mb, rows, :], pv_v[...])
        for i in range(N // NB):
            r = i * NB
            rows = slice(r, r + NB)
            ps = ssc_v[mb, rows, :]
            inv = 1.0 / (sc_v[N + r:N + r + NB, :] + ps)
            sp = sp_v[mb, rows, :].astype(F32)
            agg = (sc_v[rows, :] + ps * sp) * inv
            alpha = ps * inv
            live = (iota((NB, 1), 0) + r < cnt_ref[0, mb]).astype(F32)
            pre = agg + vecs[1:2, :] + rp_v[mb, rows, :]
            centre = pre - jnp.mean(pre, axis=1, keepdims=True)
            rstd = lax.rsqrt(jnp.mean(centre * centre, axis=1, keepdims=True) + 1e-05)
            nrm = centre * rstd
            lin = nrm * vecs[2:3, :] + vecs[3:4, :]
            e = jnp.exp(jnp.minimum(lin, 0.0))
            up = lin > 0
            x_v2 = jnp.where(up, lin, e - 1.0) * live
            cot = cot_v[mb, rows, :].astype(F32) * live
            cot_v[mb, rows, :] = x_v2.astype(BF)
            dlin = cot * jnp.where(up, 1.0, e)
            vacc[2] += fold(dlin * nrm)
            vacc[3] += fold(dlin)
            dn = dlin * vecs[2:3, :]
            dpre = rstd * (
                dn
                - jnp.mean(dn, axis=1, keepdims=True)
                - nrm * jnp.mean(dn * nrm, axis=1, keepdims=True)
            )
            vacc[1] += fold(dpre)
            loc_v[mb, rows, 2 * C:3 * C] = dpre.astype(BF)
            dagr = (dpre * inv).astype(BF)
            dagf = dagr.astype(F32)
            hi, lo = split(dagf * agg)
            big = dot(hi, eblk[...]) + dot(lo, eblk[...])
            hi, lo = split(dagf * (sp - agg))
            ds = ps * (dot(hi, eblk[...]) + dot(lo, eblk[...]))
            vacc[0] += fold(ds * sg_v[mb, rows, :].astype(F32))
            dz = ds * sga_v[mb, rows, :].astype(F32)
            loc_v[mb, rows, C:2 * C] = dz.astype(BF)
            loc_v[mb, rows, 0:C] = (alpha * dpre + dz).astype(BF)
            dtab[rows, 0:C] = dagr
            hi, lo = split(big)
            dtab[rows, C:C + 128] = (dot(hi, sel[0]) + dot(lo, sel[1])).astype(BF)

    def grad_chunk(mb, i):
        rows = edge_rows(i)
        got = dot(th[mb, rows, :], dtab[...])
        dag = got[:, 0:C]
        se = se_v[rows, :].astype(F32)
        hi, lo = split(dag * se)
        p = pv_v[rows, :].astype(F32)
        ds = p * (dot(hi, eblk[...]) + dot(lo, eblk[...]) - dot(got[:, C:C + 128].astype(BF), exp2[...]))
        vacc[0] += fold(ds * g_v[rows, :].astype(F32))
        dz = ds * ga_v[rows, :]
        eg = (p * dag + dz).astype(BF)
        rs[mb, rows, :] = eg
        fs[mb, rows, :] = dz.astype(BF)

    def backward_edges(mb):
        for i in range(NCH):
            grad_chunk(mb, i)
            if i > 0:
                send_chunk(rs, rr, mb, i - 1, -1, rs_sem, rr_sem)
        send_chunk(rs, rr, mb, NCH - 1, -1, rs_sem, rr_sem)

    most = pl.ds(0, (DEV - 1) * CAP)

    def one_batch(mb, carry):
        forward_edges(mb)
        tops(mb)
        weigh(mb)
        nodes(mb)
        pltpu.make_async_copy(cot_v.at[mb], out_hbm.at[mb], out_sem.at[mb]).start()
        pltpu.make_async_copy(fs.at[mb, most], fs.at[mb, most], fs_sem.at[mb]).wait()
        backward_edges(mb)
        return carry

    lax.fori_loop(0, MB, one_batch, 0)

    def local_grads(mb, carry):
        for i in range(N // NB):
            rows = slice(i * NB, (i + 1) * NB)
            dtgt = dot(tht[mb, rows, :], fs[mb]) + loc_v[mb, rows, C:2 * C].astype(F32)
            loc_v[mb, rows, C:2 * C] = dtgt.astype(BF)
        gacc[...] += dot_tn(x_v[mb], loc_v[mb])
        gacc[:, 0:C] += dot_tn(fr[mb], rs[mb])
        return carry

    lax.fori_loop(0, MB, local_grads, 0)

    def pack_vectors(v):
        hi = v.astype(BF).astype(F32)
        return jnp.concatenate([hi, v - hi], axis=0).astype(BF)

    def repack(v):
        cut = HALF - 16
        both = v[..., cut:cut + 8, :] + v[..., cut + 8:cut + 16, :]
        hi = both.astype(BF).astype(F32)
        last = jnp.concatenate([hi, both - hi], axis=-2)
        last = jnp.where(mc == 1, last, v[..., cut:cut + 16, :])
        return jnp.concatenate([v[..., 0:cut, :], last], axis=-2).astype(BF)

    for slot in range(3):
        g0s[:, slot * RW:(slot + 1) * RW, :] = gacc[:, slot * C:(slot + 1) * C].astype(BF).reshape(ND, RW, C)
    sums = [jnp.sum(vacc[slot], axis=0, keepdims=True) for slot in range(4)]
    packed = pack_vectors(jnp.concatenate(sums + [jnp.zeros((4, C), F32)], axis=0))
    for slot in range(ND):
        g0s[slot, 3 * RW:3 * RW + 16, :] = packed
    other = pl.ds(pl.multiple_of((1 - mc) * HALF, 16), HALF)
    pltpu.make_async_remote_copy(
        src_ref=g0s.at[:, other], dst_ref=g0r, send_sem=r_sem.at[4], recv_sem=r_sem.at[5],
        device_id=twin, device_id_type=MESH,
    ).start()

    def partials(mb, carry):
        for i in range(N // NB):
            rows = slice(i * NB, (i + 1) * NB)
            rp_v[mb, rows, :] = dot_nt(loc_v[mb, rows, C:3 * C], wcat[:, C:3 * C])
        fill_turned(srow, mb, tht)
        return carry

    partials(0, 0)
    pltpu.make_async_copy(g0r, g0r, r_sem.at[5]).wait()
    g1s[...] = repack(g0s[:, half, :].astype(F32) + g0r[...].astype(F32))

    def send_first(i, carry):
        to = lax.rem(d + i, ND)
        pltpu.make_async_remote_copy(
            src_ref=g1s.at[to], dst_ref=g1r.at[d], send_sem=r_sem.at[0], recv_sem=r_sem.at[1],
            device_id=(g, to), device_id_type=MESH,
        ).start()
        return carry

    lax.fori_loop(1, ND, send_first, 0)
    pltpu.make_async_copy(g1s.at[d], g1r.at[d], r_sem.at[1]).start()
    partials(1, 0)

    def finish(mb):
        for i in range(NCH):
            rows = pl.ds(i * EC, EC)
            pltpu.make_async_copy(rr.at[mb, rows], rr.at[mb, rows], rr_sem.at[mb, i]).wait()
        pltpu.make_async_copy(cot_v.at[mb], out_hbm.at[mb], out_sem.at[mb]).wait()

        def step(i, carry):
            rows = pl.ds(pl.multiple_of(i * NB, NB), NB)
            dsrc = (dot(tht[mb, rows, :], rr[mb]) + loc_v[mb, rows, 0:C].astype(F32)).astype(BF)
            cot_v[mb, rows, :] = (dot_nt(dsrc, wcat[:, 0:C]) + rp_v[mb, rows, :]).astype(BF)
            return carry

        lax.fori_loop(0, N // NB, step, 0)
        pltpu.make_async_copy(cot_v.at[mb], gf_hbm.at[mb], out_sem.at[mb]).start()

    finish(0)

    pltpu.make_async_copy(g1r, g1r, r_sem.at[1]).wait()
    g2s[...] = repack(jnp.sum(g1r[...].astype(F32), axis=0))

    def send_second(i, carry):
        pltpu.make_async_remote_copy(
            src_ref=g2s, dst_ref=g2r.at[g], send_sem=r_sem.at[2], recv_sem=r_sem.at[3],
            device_id=(lax.rem(g + i, NG), d), device_id_type=MESH,
        ).start()
        return carry

    lax.fori_loop(1, NG, send_second, 0)
    pltpu.make_async_copy(g2s, g2r.at[g], r_sem.at[3]).start()

    for mb in range(1, MB):
        finish(mb)

    pltpu.make_async_copy(g2r, g2r, r_sem.at[3]).wait()
    for side in range(2):
        total = g2r[side].astype(F32)
        for slot in range(1, X):
            total = total + g2r[2 * slot + side].astype(F32)
        small_ref[side * HALF:(side + 1) * HALF, :] = total
    tail = small_ref[3 * RW:3 * RW + 8, :] + small_ref[3 * RW + 8:3 * RW + 16, :]
    small_ref[3 * RW:3 * RW + 8, :] = pltpu.roll(tail, lax.rem(C - d * RW, C), 1)

    for mb in range(MB):
        pltpu.make_async_copy(cot_v.at[mb], gf_hbm.at[mb], out_sem.at[mb]).wait()
        pltpu.make_async_copy(rs.at[mb, most], rs.at[mb, most], rs_sem.at[mb]).wait()
    pltpu.make_async_copy(mine, mine, w_sem.at[2]).wait()
    others = pl.ds(0, ND - 1)
    mine = wall.at[others, half]
    pltpu.make_async_copy(mine, mine, w_sem.at[0]).wait()
    pltpu.make_async_copy(g0r, g0r, r_sem.at[4]).wait()
    pltpu.make_async_copy(g1s.at[others], g1s.at[others], r_sem.at[0]).wait()
    others = pl.ds(0, NG - 1)
    pltpu.make_async_copy(g2r.at[others], g2r.at[others], r_sem.at[2]).wait()


def hand_on(RW, out_in, gf_in, small_in, out_hbm, gf_hbm, gws, gwt, gwr, v0, v1, v2, v3, held, sems):
    MB = out_in.shape[0]
    loads, stores = [], []
    for mb in range(MB):
        for src, dst in ((out_in, out_hbm), (gf_in, gf_hbm)):
            slot = len(loads)
            loads.append(pltpu.make_async_copy(src.at[mb], held.at[slot], sems.at[0, slot]))
            stores.append(pltpu.make_async_copy(held.at[slot], dst.at[mb], sems.at[1, slot]))
    for load in loads:
        load.start()
    for slot, dst in enumerate((gws, gwt, gwr)):
        dst[...] = small_in[slot * RW:(slot + 1) * RW, :]
    for slot, dst in enumerate((v0, v1, v2, v3)):
        dst[...] = small_in[3 * RW + slot:3 * RW + slot + 1, 0:RW]
    for load, store in zip(loads, stores):
        load.wait()
        store.start()
    for store in stores:
        store.wait()


def local(
    shape,
    features, w_source, w_target, w_residual, attention, out_bias, norm_gain, norm_shift,
    node_count, edge_src, edge_tgt, cotangent,
):
    NG, ND = shape
    X = NG // 2
    Y = 1
    while Y * Y < ND:
        Y *= 2
    Z = ND // Y
    MB, N, C = features.shape
    CAP = edge_src.shape[3]
    DEV = NG * ND
    E = DEV * CAP
    EC = min(256, E // 2)
    NCH = E // EC
    RW = C // ND
    PK = 3 * RW + 16
    groups = N // 64
    vmem = pl.BlockSpec(memory_space=pltpu.VMEM)
    hbm = pl.BlockSpec(memory_space=pl.ANY)
    smem = pl.BlockSpec(memory_space=pltpu.SMEM)
    cfg = (NG, ND, X, Y, Z, N, CAP, MB, EC)
    V = pltpu.VMEM
    DMA = pltpu.SemaphoreType.DMA
    I16 = jnp.int16
    wide = jax.ShapeDtypeStruct((MB, N, C), BF)
    block = jax.ShapeDtypeStruct((RW, C), F32)
    line = jax.ShapeDtypeStruct((1, RW), F32)
    result, grad_rows, small = pl.pallas_call(
        functools.partial(kernel, cfg),
        out_shape=(wide, wide, jax.ShapeDtypeStruct((PK, C), F32)),
        in_specs=[smem] + [vmem] * 6 + [hbm] * 5,
        out_specs=(hbm, hbm, vmem),
        scratch_shapes=[
            V((MB, N, C), BF), V((MB, N, C), BF),
            V((MB, E, C), BF), V((MB, E, C), BF), V((MB, E, C), BF), V((MB, E, C), BF),
            V((PK, C), BF), V((ND, PK, C), BF), V((C, 3 * C), BF),
            V((2 * MB, DEV, 2 * CAP), BF), V((MB, E, 128), F32),
            V((MB, NCH, 16, EC), I16), V((MB, NCH, 16, EC), I16),
            V((MB, E, N), BF), V((MB, N, E), BF),
            V((E, C), BF), V((E, C), BF), V((E, C), F32), V((max(E, 2 * N), C), F32), V((E, C), BF),
            V((MB, N, C), BF), V((MB, N, C), BF), V((MB, N, C), F32),
            V((MB, N, C), BF), V((MB, N, C), F32), V((MB, N, C), F32),
            V((N, 128), BF), V((2 * groups, 8, 128), F32),
            V((N, C + 128), BF), V((MB, N, 3 * C), BF),
            V((C, C), BF), V((C, C), BF), V((128, C), BF), V((128, C), BF), V((2, C, 128), BF),
            V((8, C), F32), V((4, 8, C), F32), V((C, 3 * C), F32),
            V((ND, PK, C), BF), V((ND, PK // 2, C), BF), V((ND, PK // 2, C), BF),
            V((ND, PK // 2, C), BF), V((PK // 2, C), BF), V((NG, PK // 2, C), BF),
            DMA((5,)), DMA((MB,)), DMA((MB, NCH)), DMA((MB,)), DMA((MB, NCH)),
            DMA((4,)), DMA((6,)), DMA((MB,)),
        ],
        compiler_params=pltpu.CompilerParams(
            collective_id=0, has_side_effects=True, vmem_limit_bytes=62 * 2**20
        ),
        cost_estimate=pl.CostEstimate(
            flops=20 * MB * E * N * C, bytes_accessed=10 * MB * N * C, transcendentals=4 * MB * E * C
        ),
    )(
        jnp.swapaxes(node_count, 0, 1), jnp.swapaxes(edge_src, 2, 3), jnp.swapaxes(edge_tgt, 2, 3),
        attention.reshape(1, RW), out_bias.reshape(1, RW), norm_gain.reshape(1, RW), norm_shift.reshape(1, RW),
        features, cotangent, w_source, w_target, w_residual,
    )
    outs = pl.pallas_call(
        functools.partial(hand_on, RW),
        out_shape=(wide, wide, block, block, block, line, line, line, line),
        in_specs=[hbm, hbm, vmem],
        out_specs=(hbm, hbm) + (vmem,) * 7,
        scratch_shapes=[V((2 * MB, N, C), BF), DMA((2, 2 * MB))],
    )(result, grad_rows, small)
    return outs[:5] + tuple(v.reshape(RW) for v in outs[5:])


def solution(mesh):
    shape = (mesh.shape["grp"], mesh.shape["dev"])
    return jax.shard_map(
        functools.partial(local, shape),
        mesh=mesh,
        in_specs=(
            P(None, ("grp", "dev"), None),
            P("dev", None),
            P("dev", None),
            P("dev", None),
            P("dev"),
            P("dev"),
            P("dev"),
            P("dev"),
            P(None, ("grp", "dev")),
            P(None, ("grp", "dev"), None, None),
            P(None, ("grp", "dev"), None, None),
            P(None, ("grp", "dev"), None),
        ),
        out_specs=(
            P(None, ("grp", "dev"), None),
            P(None, ("grp", "dev"), None),
            P("dev", None),
            P("dev", None),
            P("dev", None),
            P("dev"),
            P("dev"),
            P("dev"),
            P("dev"),
        ),
        check_vma=False,
    )
```

```python
import functools

import jax
import jax.numpy as jnp
from jax import lax
from jax.experimental import pallas as pl
from jax.experimental.pallas import tpu as pltpu
from jax.sharding import PartitionSpec as P

MESH = pl.DeviceIdType.MESH
BF = jnp.bfloat16
F32 = jnp.float32
H = 4
LOWEST = -1e30
C0 = 0.7978845608028654
C1 = 0.044715


def dot(a, b):
    return jnp.dot(a, b, preferred_element_type=F32)


def dot_nt(a, b):
    return lax.dot_general(a, b, (((1,), (1,)), ((), ())), preferred_element_type=F32)


def dot_tn(a, b):
    return lax.dot_general(a, b, (((0,), (0,)), ((), ())), preferred_element_type=F32)


def iota(shape, axis, kind=jnp.int32):
    return lax.broadcasted_iota(kind, shape, axis)


def gelu_pair(z):
    zz = z * z
    t = jnp.tanh(z * (C0 + (C0 * C1) * zz))
    half = 0.5 * z
    g = half + half * t
    gp = (0.5 + 0.5 * t) + (half - half * (t * t)) * (C0 + (3.0 * C0 * C1) * zz)
    return g, gp


def split(v):
    hi = v.astype(BF)
    return hi, (v - hi.astype(F32)).astype(BF)


def kernel(
    cfg,
    cnt_ref, esrc_ref, etgt_ref, att_ref, bias_ref, gain_ref, shift_ref,
    x_hbm, cot_hbm, ws_hbm, wt_hbm, wr_hbm,
    out_hbm, gf_hbm, small_ref,
    x_v, cot_v, fs, fr, rs, rr, wsend, wall, wcat,
    lists, tcolf, trow, srow, th, tht,
    se_v, g_v, ga_v, sc_v, pv_v, sp_v, tp_v, rp_v, sg_v, sga_v, ssc_v, mtab, mx_v,
    dtab, loc_v, a2, eblk, exp2, spread, sel, vecs, vacc, gacc,
    g0s, g0r, g1s, g1r, g2s, g2r,
    in_sem, fs_sem, fr_sem, rs_sem, rr_sem, w_sem, r_sem, out_sem,
):
    NG, ND, X, Y, Z, N, CAP, MB, EC = cfg
    C = 256
    DEV = NG * ND
    E = DEV * CAP
    NCH = E // EC
    PER = EC // CAP
    RW = C // ND
    PK = 3 * RW + 16
    HALF = PK // 2
    NB = min(256, N)
    W8 = 2 * X
    STEP = 1
    g, d = lax.axis_index("grp"), lax.axis_index("dev")
    mx, mc = lax.div(g, 2), lax.rem(g, 2)
    my, mz = lax.div(d, Z), lax.rem(d, Z)
    twin = (mx * 2 + 1 - mc, d)

    def place(i, q, sign):
        a, k = q // 2, q % 2
        if isinstance(i, int):
            b, c = i % Y, i // Y
            dy, dz = (a + b) % Y, (a + b + c) % Z
        else:
            b, c = lax.rem(i, Y), lax.div(i, Y)
            dy, dz = lax.rem(a + b, Y), lax.rem(a + b + c, Z)
        if sign > 0:
            px, py, pz = mx + a, my + dy, mz + dz
        else:
            px, py, pz = mx + (X - a), my + (Y - dy), mz + (Z - dz)
        return (
            lax.rem(px, X) * 2 + lax.rem(mc + k, 2),
            lax.rem(py, Y) * Z + lax.rem(pz, Z),
        )

    loads = [
        pltpu.make_async_copy(x_hbm, x_v, in_sem.at[0]),
        pltpu.make_async_copy(ws_hbm, wsend.at[pl.ds(0, RW)], in_sem.at[1]),
        pltpu.make_async_copy(wt_hbm, wsend.at[pl.ds(RW, RW)], in_sem.at[2]),
        pltpu.make_async_copy(wr_hbm, wsend.at[pl.ds(2 * RW, RW)], in_sem.at[3]),
        pltpu.make_async_copy(cot_hbm, cot_v, in_sem.at[4]),
    ]
    for load in loads:
        load.start()

    barrier = pltpu.get_barrier_semaphore()

    def greet(i, q):
        pl.semaphore_signal(barrier, inc=1, device_id=place(i, q, 1), device_id_type=MESH)

    for j in range(1, DEV):
        greet(j // W8, j % W8)
    rep = (iota((RW, C), 1) % RW == iota((RW, C), 0)).astype(F32).astype(BF)
    here = (iota((8, C), 1) // RW == d)
    rows = [jnp.where(here, dot(jnp.broadcast_to(ref[...], (8, RW)), rep), 0.0)
            for ref in (att_ref, bias_ref, gain_ref, shift_ref)]
    line = iota((8, C), 0)
    placed = jnp.zeros((8, C), F32)
    for slot in range(4):
        placed = jnp.where(line == slot, rows[slot], placed)
    wsend[pl.ds(3 * RW, 16), :] = jnp.concatenate([placed, jnp.zeros((8, C), F32)], axis=0).astype(BF)

    def order(sign):
        j = iota((DEV, DEV), 0)
        k = j & 1
        a = (j >> 1) & (X - 1)
        b = (j // W8) & (Y - 1)
        c = j // (W8 * Y)
        dx, dy, dz = a, (a + b) & (Y - 1), (a + b + c) & (Z - 1)
        px = (mx + X + sign * dx) & (X - 1)
        py = (my + Y + sign * dy) & (Y - 1)
        pz = (mz + Z + sign * dz) & (Z - 1)
        dev = (px * 2 + ((mc + k) & 1)) * ND + py * Z + pz
        return (dev == iota((DEV, DEV), 1)).astype(F32).astype(BF)

    LB = 2 * CAP

    def list_of(slot, sign, tabs, mb):
        parts = jnp.concatenate([tabs[mb, 0] >> 5, tabs[mb, 0] & 31], axis=0)
        lists[slot] = dot_nt(order(sign), parts.astype(F32).astype(BF)).astype(BF)

    def expand(slot, i):
        e = iota((EC, DEV), 0) + i * EC
        pairs = ((e // CAP) == iota((EC, DEV), 1)).astype(F32).astype(BF)
        own = (iota((EC, LB), 0) & (CAP - 1)) == (iota((EC, LB), 1) & (CAP - 1))
        kept = jnp.where(own, dot(pairs, lists[slot]), 0.0).astype(BF)
        widen = jnp.where(iota((LB, 128), 0) < CAP, 32.0, 1.0).astype(BF)
        turn = jnp.where(iota((16, LB), 1) < CAP, 32.0, 1.0).astype(BF)
        return dot(kept, widen), dot_nt(turn, kept).astype(jnp.int32).astype(jnp.int16)

    def onehot_rows(col):
        wide = jnp.concatenate([col] * (N // 128), axis=1)
        return jnp.where(wide == iota(wide.shape, 1, jnp.int16), jnp.ones((), BF), jnp.zeros((), BF))

    def fill_turned(row, mb, dst):
        def step(i, carry):
            r = pl.multiple_of(i * 128, 128)
            ids = iota((128, EC), 0, jnp.int16) + (i * 128).astype(jnp.int16)
            for q in range(NCH):
                wide = jnp.concatenate([row[mb, q]] * 8, axis=0)
                dst[mb, pl.ds(r, 128), q * EC:(q + 1) * EC] = jnp.where(
                    wide == ids, jnp.ones((), BF), jnp.zeros((), BF)
                )
            return carry

        lax.fori_loop(0, N // 128, step, 0)

    def send_block(src, dst, mb, j, sign, ssem, rsem):
        rows = pl.ds(j * CAP, CAP)
        pltpu.make_async_remote_copy(
            src_ref=src.at[mb, rows], dst_ref=dst.at[mb, rows],
            send_sem=ssem.at[mb], recv_sem=rsem.at[mb, j // PER],
            device_id=place(j // W8, j % W8, sign), device_id_type=MESH,
        ).start()

    def send_chunk(src, dst, mb, i, sign, ssem, rsem):
        if i == 0:
            pltpu.make_async_copy(
                src.at[mb, pl.ds(0, CAP)], dst.at[mb, pl.ds(0, CAP)], rsem.at[mb, 0]
            ).start()
        for j in range(max(1, i * PER), (i + 1) * PER):
            send_block(src, dst, mb, j, sign, ssem, rsem)

    for mb in range(MB):
        list_of(mb, 1, esrc_ref, mb)
    loads[0].wait()
    pl.semaphore_wait(barrier, DEV - 1)

    def outgoing(mb, carry):
        for i in range(NCH):
            wide, flat = expand(mb, i)
            srow[mb, i] = flat
            hot = onehot_rows(wide.astype(jnp.int32).astype(jnp.int16))
            fs[mb, i * EC:(i + 1) * EC, :] = dot(hot, x_v[mb]).astype(BF)
            if i > 0:
                send_chunk(fs, fr, mb, i - 1, 1, fs_sem, fr_sem)
        send_chunk(fs, fr, mb, NCH - 1, 1, fs_sem, fr_sem)
        return carry

    for load in loads[1:4]:
        load.wait()
    half = pl.ds(pl.multiple_of(mc * HALF, 16), HALF)

    def send_weights(i, carry):
        pltpu.make_async_remote_copy(
            src_ref=wsend.at[half], dst_ref=wall.at[d, half],
            send_sem=w_sem.at[0], recv_sem=w_sem.at[1],
            device_id=(g, lax.rem(d + i, ND)), device_id_type=MESH,
        ).start()
        return carry

    lax.fori_loop(1, ND, send_weights, 0)
    pltpu.make_async_copy(wsend.at[half], wall.at[d, half], w_sem.at[1]).start()

    outgoing(0, 0)

    mine = wall.at[:, half]
    pltpu.make_async_copy(mine, mine, w_sem.at[1]).wait()
    pltpu.make_async_remote_copy(
        src_ref=mine, dst_ref=mine, send_sem=w_sem.at[2], recv_sem=w_sem.at[3],
        device_id=twin, device_id_type=MESH,
    ).start()
    for mb in range(1, MB):
        outgoing(mb, 0)

    for mb in range(MB):
        list_of(MB + mb, -1, etgt_ref, mb)

    def incoming(mb, carry):
        for i in range(NCH):
            wide, flat = expand(MB + mb, i)
            rows = slice(i * EC, (i + 1) * EC)
            tcolf[mb, rows, :] = wide
            th[mb, rows, :] = onehot_rows(wide.astype(jnp.int32).astype(jnp.int16))
            trow[mb, i] = flat
        fill_turned(trow, mb, tht)
        return carry

    lax.fori_loop(0, MB, incoming, 0)
    same = (iota((C, C), 0) // 64) == (iota((C, C), 1) // 64)
    eblk[...] = same.astype(F32).astype(BF)
    lane = iota((128, C), 0)
    head = iota((128, C), 1) // 64
    exp2[...] = ((lane < 8) & ((lane & 3) == head)).astype(F32).astype(BF)
    groups = N // 64
    r = lane & 63
    at = 2 * ((r & 31) // groups) + r // 32
    spread[...] = ((at == head) & ((r & 31) < 2 * groups)).astype(F32).astype(BF)
    pick = iota((C, 128), 0)
    slot = iota((C, 128), 1)
    sel[0] = ((pick == 64 * slot) & (slot < 4)).astype(F32).astype(BF)
    sel[1] = ((pick == 64 * (slot - 4)) & (slot >= 4) & (slot < 8)).astype(F32).astype(BF)
    vacc[...] = jnp.zeros_like(vacc)
    gacc[...] = jnp.zeros_like(gacc)

    pltpu.make_async_copy(mine, mine, w_sem.at[3]).wait()
    for slot in range(3):
        wcat[:, slot * C:(slot + 1) * C] = wall[:, slot * RW:(slot + 1) * RW, :].reshape(C, C)
    vectors = jnp.sum(wall[:, 3 * RW:3 * RW + 16, :].astype(F32), axis=0)
    vecs[...] = vectors[0:8, :]
    att_col = jnp.transpose(jnp.broadcast_to(vecs[0:1, :], (C, C)))
    a2[...] = jnp.where(same, att_col, 0.0).astype(BF)

    def project(i, carry):
        mb, part = lax.div(i, N // NB), lax.rem(i, N // NB)
        rows = pl.ds(pl.multiple_of(part * NB, NB), NB)
        proj = dot(x_v[mb, rows, :], wcat[...])
        sp = proj[:, 0:C].astype(BF)
        tp = proj[:, C:2 * C]
        sp_v[mb, rows, :] = sp
        tp_v[mb, rows, :] = tp.astype(BF)
        rp_v[mb, rows, :] = proj[:, 2 * C:3 * C]
        gs, gp = gelu_pair(sp.astype(F32) + tp)
        hi, lo = split(gs)
        sg_v[mb, rows, :] = hi
        sga_v[mb, rows, :] = gp * vecs[0:1, :]
        ssc_v[mb, rows, :] = dot(hi, a2[...]) + dot(lo, a2[...])
        return carry

    lax.fori_loop(0, MB * (N // NB), project, 0)
    loads[4].wait()

    def fold(v):
        return jnp.sum(v.reshape(v.shape[0] // 8, 8, v.shape[1]), axis=0)

    def edge_rows(i):
        return slice(i * EC, (i + 1) * EC)

    def score_chunk(mb, i):
        rows = edge_rows(i)
        se = dot(fr[mb, rows, :], wcat[:, 0:C]).astype(BF)
        se_v[rows, :] = se
        z = se.astype(F32) + dot(th[mb, rows, :], tp_v[mb])
        ge, gp = gelu_pair(z)
        hi, lo = split(ge)
        g_v[rows, :] = hi
        ga_v[rows, :] = gp * vecs[0:1, :]
        sc_v[rows, :] = dot(hi, a2[...]) + dot(lo, a2[...])

    def sweep_chunk(mb, i):
        low = (iota((64, 128), 1) & 63).astype(F32)
        for q in range(EC // 64):
            part = slice(i * EC + q * 64, i * EC + (q + 1) * 64)
            tgt = tcolf[mb, part, :]
            s0, s1 = sc_v[part, 0:128], sc_v[part, 128:256]
            for grp in range(groups):
                hit = tgt == low + (64.0 * grp)
                for side, s in enumerate((s0, s1)):
                    top = jnp.max(jnp.where(hit, s, LOWEST).reshape(8, 8, 128), axis=0)
                    at = side * groups + grp
                    mx_v[at] = jnp.maximum(mx_v[at], top)

    def forward_edges(mb):
        mx_v[...] = jnp.full(mx_v.shape, LOWEST, F32)
        for i in range(NCH):
            if i % STEP == 0:
                for k in range(i, min(i + STEP, NCH)):
                    part = fr.at[mb, pl.ds(k * EC, EC)]
                    pltpu.make_async_copy(part, part, fr_sem.at[mb, k]).wait()
            score_chunk(mb, i)
            if i > 0:
                sweep_chunk(mb, i - 1)
        sweep_chunk(mb, NCH - 1)

    def tops(mb):
        tall = [mx_v[at] for at in range(2 * groups)]
        for shift in (4, 2, 1):
            tall = [jnp.maximum(v, pltpu.roll(v, shift, 0)) for v in tall]
        sub = iota((8, 128), 0)
        best = []
        for at in range(0, 2 * groups, 8):
            row = tall[at]
            for k in range(1, min(8, 2 * groups - at)):
                row = jnp.where(sub == k, tall[at + k], row)
            best.append(row)
        best = jnp.concatenate(best + [jnp.zeros((128 - 8 * len(best), 128), F32)], axis=0)
        turned = jnp.transpose(best)
        both = turned[0:64, :] + pltpu.roll(turned[64:128, :], 32, 1)
        hi = both.astype(BF).astype(F32)
        table = hi + pltpu.roll(both - hi, 64, 1)
        for i in range(N // NB):
            rows = slice(i * NB, (i + 1) * NB)
            whose = iota((NB, 128), 0) // 64 + i * (NB // 64)
            mine = jnp.concatenate([table] * (NB // 64), axis=0)
            mine = jnp.where((iota((NB, 128), 1) & (groups - 1)) == whose, mine, 0.0).astype(BF)
            own = ssc_v[mb, rows, :]
            hi, lo = split(jnp.maximum(dot(mine, spread[...]), own))
            ssc_v[mb, rows, :] = jnp.exp(own - (hi.astype(F32) + lo.astype(F32)))
            mtab[rows, :] = (dot(hi, sel[0]) + dot(lo, sel[1])).astype(BF)

    def weigh(mb):
        for i in range(NCH):
            rows = edge_rows(i)
            me = dot(th[mb, rows, :], mtab[...]).astype(BF)
            live = tcolf[mb, rows, :] >= 0.0
            live = jnp.concatenate([live, live], axis=1)
            p = jnp.where(live, jnp.exp(sc_v[rows, :] - dot(me, exp2[...])), 0.0)
            rs[mb, rows, :] = (p * se_v[rows, :].astype(F32)).astype(BF)
            pv_v[rows, :] = p.astype(BF)

    def nodes(mb):
        for i in range(N // NB):
            rows = slice(i * NB, (i + 1) * NB)
            sc_v[rows, :] = dot(tht[mb, rows, :], rs[mb])
            sc_v[N + i * NB:N + (i + 1) * NB, :] = dot(tht[mb, rows, :], pv_v[...])
        for i in range(N // NB):
            r = i * NB
            rows = slice(r, r + NB)
            ps = ssc_v[mb, rows, :]
            inv = 1.0 / (sc_v[N + r:N + r + NB, :] + ps)
            sp = sp_v[mb, rows, :].astype(F32)
            agg = (sc_v[rows, :] + ps * sp) * inv
            alpha = ps * inv
            live = (iota((NB, 1), 0) + r < cnt_ref[0, mb]).astype(F32)
            pre = agg + vecs[1:2, :] + rp_v[mb, rows, :]
            centre = pre - jnp.mean(pre, axis=1, keepdims=True)
            rstd = lax.rsqrt(jnp.mean(centre * centre, axis=1, keepdims=True) + 1e-05)
            nrm = centre * rstd
            lin = nrm * vecs[2:3, :] + vecs[3:4, :]
            e = jnp.exp(jnp.minimum(lin, 0.0))
            up = lin > 0
            x_v2 = jnp.where(up, lin, e - 1.0) * live
            cot = cot_v[mb, rows, :].astype(F32) * live
            cot_v[mb, rows, :] = x_v2.astype(BF)
            dlin = cot * jnp.where(up, 1.0, e)
            vacc[2] += fold(dlin * nrm)
            vacc[3] += fold(dlin)
            dn = dlin * vecs[2:3, :]
            dpre = rstd * (
                dn
                - jnp.mean(dn, axis=1, keepdims=True)
                - nrm * jnp.mean(dn * nrm, axis=1, keepdims=True)
            )
            vacc[1] += fold(dpre)
            loc_v[mb, rows, 2 * C:3 * C] = dpre.astype(BF)
            dagr = (dpre * inv).astype(BF)
            dagf = dagr.astype(F32)
            hi, lo = split(dagf * agg)
            big = dot(hi, eblk[...]) + dot(lo, eblk[...])
            hi, lo = split(dagf * (sp - agg))
            ds = ps * (dot(hi, eblk[...]) + dot(lo, eblk[...]))
            vacc[0] += fold(ds * sg_v[mb, rows, :].astype(F32))
            dz = ds * sga_v[mb, rows, :].astype(F32)
            loc_v[mb, rows, C:2 * C] = dz.astype(BF)
            loc_v[mb, rows, 0:C] = (alpha * dpre + dz).astype(BF)
            dtab[rows, 0:C] = dagr
            hi, lo = split(big)
            dtab[rows, C:C + 128] = (dot(hi, sel[0]) + dot(lo, sel[1])).astype(BF)

    def grad_chunk(mb, i):
        rows = edge_rows(i)
        got = dot(th[mb, rows, :], dtab[...])
        dag = got[:, 0:C]
        se = se_v[rows, :].astype(F32)
        hi, lo = split(dag * se)
        p = pv_v[rows, :].astype(F32)
        ds = p * (dot(hi, eblk[...]) + dot(lo, eblk[...]) - dot(got[:, C:C + 128].astype(BF), exp2[...]))
        vacc[0] += fold(ds * g_v[rows, :].astype(F32))
        dz = ds * ga_v[rows, :]
        eg = (p * dag + dz).astype(BF)
        rs[mb, rows, :] = eg
        fs[mb, rows, :] = dz.astype(BF)

    def backward_edges(mb):
        for i in range(NCH):
            grad_chunk(mb, i)
            if i > 0:
                send_chunk(rs, rr, mb, i - 1, -1, rs_sem, rr_sem)
        send_chunk(rs, rr, mb, NCH - 1, -1, rs_sem, rr_sem)

    most = pl.ds(0, (DEV - 1) * CAP)

    def one_batch(mb, carry):
        forward_edges(mb)
        tops(mb)
        weigh(mb)
        nodes(mb)
        pltpu.make_async_copy(cot_v.at[mb], out_hbm.at[mb], out_sem.at[mb]).start()
        pltpu.make_async_copy(fs.at[mb, most], fs.at[mb, most], fs_sem.at[mb]).wait()
        backward_edges(mb)
        return carry

    lax.fori_loop(0, MB, one_batch, 0)

    def local_grads(mb, carry):
        for i in range(N // NB):
            rows = slice(i * NB, (i + 1) * NB)
            dtgt = dot(tht[mb, rows, :], fs[mb]) + loc_v[mb, rows, C:2 * C].astype(F32)
            loc_v[mb, rows, C:2 * C] = dtgt.astype(BF)
        gacc[...] += dot_tn(x_v[mb], loc_v[mb])
        gacc[:, 0:C] += dot_tn(fr[mb], rs[mb])
        return carry

    lax.fori_loop(0, MB, local_grads, 0)

    def pack_vectors(v):
        hi = v.astype(BF).astype(F32)
        return jnp.concatenate([hi, v - hi], axis=0).astype(BF)

    def repack(v):
        cut = HALF - 16
        both = v[..., cut:cut + 8, :] + v[..., cut + 8:cut + 16, :]
        hi = both.astype(BF).astype(F32)
        last = jnp.concatenate([hi, both - hi], axis=-2)
        last = jnp.where(mc == 1, last, v[..., cut:cut + 16, :])
        return jnp.concatenate([v[..., 0:cut, :], last], axis=-2).astype(BF)

    for slot in range(3):
        g0s[:, slot * RW:(slot + 1) * RW, :] = gacc[:, slot * C:(slot + 1) * C].astype(BF).reshape(ND, RW, C)
    sums = [jnp.sum(vacc[slot], axis=0, keepdims=True) for slot in range(4)]
    packed = pack_vectors(jnp.concatenate(sums + [jnp.zeros((4, C), F32)], axis=0))
    for slot in range(ND):
        g0s[slot, 3 * RW:3 * RW + 16, :] = packed
    other = pl.ds(pl.multiple_of((1 - mc) * HALF, 16), HALF)
    pltpu.make_async_remote_copy(
        src_ref=g0s.at[:, other], dst_ref=g0r, send_sem=r_sem.at[4], recv_sem=r_sem.at[5],
        device_id=twin, device_id_type=MESH,
    ).start()

    def partials(mb, carry):
        for i in range(N // NB):
            rows = slice(i * NB, (i + 1) * NB)
            rp_v[mb, rows, :] = dot_nt(loc_v[mb, rows, C:3 * C], wcat[:, C:3 * C])
        fill_turned(srow, mb, tht)
        return carry

    partials(0, 0)
    pltpu.make_async_copy(g0r, g0r, r_sem.at[5]).wait()
    g1s[...] = repack(g0s[:, half, :].astype(F32) + g0r[...].astype(F32))

    def send_first(i, carry):
        to = lax.rem(d + i, ND)
        pltpu.make_async_remote_copy(
            src_ref=g1s.at[to], dst_ref=g1r.at[d], send_sem=r_sem.at[0], recv_sem=r_sem.at[1],
            device_id=(g, to), device_id_type=MESH,
        ).start()
        return carry

    lax.fori_loop(1, ND, send_first, 0)
    pltpu.make_async_copy(g1s.at[d], g1r.at[d], r_sem.at[1]).start()
    partials(1, 0)

    def finish(mb):
        for i in range(NCH):
            rows = pl.ds(i * EC, EC)
            pltpu.make_async_copy(rr.at[mb, rows], rr.at[mb, rows], rr_sem.at[mb, i]).wait()
        pltpu.make_async_copy(cot_v.at[mb], out_hbm.at[mb], out_sem.at[mb]).wait()

        def step(i, carry):
            rows = pl.ds(pl.multiple_of(i * NB, NB), NB)
            dsrc = (dot(tht[mb, rows, :], rr[mb]) + loc_v[mb, rows, 0:C].astype(F32)).astype(BF)
            cot_v[mb, rows, :] = (dot_nt(dsrc, wcat[:, 0:C]) + rp_v[mb, rows, :]).astype(BF)
            return carry

        lax.fori_loop(0, N // NB, step, 0)
        pltpu.make_async_copy(cot_v.at[mb], gf_hbm.at[mb], out_sem.at[mb]).start()

    finish(0)

    pltpu.make_async_copy(g1r, g1r, r_sem.at[1]).wait()
    g2s[...] = repack(jnp.sum(g1r[...].astype(F32), axis=0))

    def send_second(i, carry):
        pltpu.make_async_remote_copy(
            src_ref=g2s, dst_ref=g2r.at[g], send_sem=r_sem.at[2], recv_sem=r_sem.at[3],
            device_id=(lax.rem(g + i, NG), d), device_id_type=MESH,
        ).start()
        return carry

    lax.fori_loop(1, NG, send_second, 0)
    pltpu.make_async_copy(g2s, g2r.at[g], r_sem.at[3]).start()

    for mb in range(1, MB):
        finish(mb)

    pltpu.make_async_copy(g2r, g2r, r_sem.at[3]).wait()
    for side in range(2):
        total = g2r[side].astype(F32)
        for slot in range(1, X):
            total = total + g2r[2 * slot + side].astype(F32)
        small_ref[side * HALF:(side + 1) * HALF, :] = total
    tail = small_ref[3 * RW:3 * RW + 8, :] + small_ref[3 * RW + 8:3 * RW + 16, :]
    small_ref[3 * RW:3 * RW + 8, :] = pltpu.roll(tail, lax.rem(C - d * RW, C), 1)

    for mb in range(MB):
        pltpu.make_async_copy(cot_v.at[mb], gf_hbm.at[mb], out_sem.at[mb]).wait()
        pltpu.make_async_copy(rs.at[mb, most], rs.at[mb, most], rs_sem.at[mb]).wait()
    pltpu.make_async_copy(mine, mine, w_sem.at[2]).wait()
    others = pl.ds(0, ND - 1)
    mine = wall.at[others, half]
    pltpu.make_async_copy(mine, mine, w_sem.at[0]).wait()
    pltpu.make_async_copy(g0r, g0r, r_sem.at[4]).wait()
    pltpu.make_async_copy(g1s.at[others], g1s.at[others], r_sem.at[0]).wait()
    others = pl.ds(0, NG - 1)
    pltpu.make_async_copy(g2r.at[others], g2r.at[others], r_sem.at[2]).wait()


def hand_on(RW, out_in, gf_in, small_in, out_hbm, gf_hbm, gws, gwt, gwr, v0, v1, v2, v3, held, sems):
    MB = out_in.shape[0]
    loads, stores = [], []
    for mb in range(MB):
        for src, dst in ((out_in, out_hbm), (gf_in, gf_hbm)):
            slot = len(loads)
            loads.append(pltpu.make_async_copy(src.at[mb], held.at[slot], sems.at[0, slot]))
            stores.append(pltpu.make_async_copy(held.at[slot], dst.at[mb], sems.at[1, slot]))
    for load in loads:
        load.start()
    for slot, dst in enumerate((gws, gwt, gwr)):
        dst[...] = small_in[slot * RW:(slot + 1) * RW, :]
    for slot, dst in enumerate((v0, v1, v2, v3)):
        dst[...] = small_in[3 * RW + slot:3 * RW + slot + 1, 0:RW]
    for load, store in zip(loads, stores):
        load.wait()
        store.start()
    for store in stores:
        store.wait()


def local(
    shape,
    features, w_source, w_target, w_residual, attention, out_bias, norm_gain, norm_shift,
    node_count, edge_src, edge_tgt, cotangent,
):
    NG, ND = shape
    X = NG // 2
    Y = 1
    while Y * Y < ND:
        Y *= 2
    Z = ND // Y
    MB, N, C = features.shape
    CAP = edge_src.shape[3]
    DEV = NG * ND
    E = DEV * CAP
    EC = min(256, E // 2)
    NCH = E // EC
    RW = C // ND
    PK = 3 * RW + 16
    groups = N // 64
    vmem = pl.BlockSpec(memory_space=pltpu.VMEM)
    hbm = pl.BlockSpec(memory_space=pl.ANY)
    smem = pl.BlockSpec(memory_space=pltpu.SMEM)
    cfg = (NG, ND, X, Y, Z, N, CAP, MB, EC)
    V = pltpu.VMEM
    DMA = pltpu.SemaphoreType.DMA
    I16 = jnp.int16
    wide = jax.ShapeDtypeStruct((MB, N, C), BF)
    block = jax.ShapeDtypeStruct((RW, C), F32)
    line = jax.ShapeDtypeStruct((1, RW), F32)
    result, grad_rows, small = pl.pallas_call(
        functools.partial(kernel, cfg),
        out_shape=(wide, wide, jax.ShapeDtypeStruct((PK, C), F32)),
        in_specs=[smem] + [vmem] * 6 + [hbm] * 5,
        out_specs=(hbm, hbm, vmem),
        scratch_shapes=[
            V((MB, N, C), BF), V((MB, N, C), BF),
            V((MB, E, C), BF), V((MB, E, C), BF), V((MB, E, C), BF), V((MB, E, C), BF),
            V((PK, C), BF), V((ND, PK, C), BF), V((C, 3 * C), BF),
            V((2 * MB, DEV, 2 * CAP), BF), V((MB, E, 128), F32),
            V((MB, NCH, 16, EC), I16), V((MB, NCH, 16, EC), I16),
            V((MB, E, N), BF), V((MB, N, E), BF),
            V((E, C), BF), V((E, C), BF), V((E, C), F32), V((max(E, 2 * N), C), F32), V((E, C), BF),
            V((MB, N, C), BF), V((MB, N, C), BF), V((MB, N, C), F32),
            V((MB, N, C), BF), V((MB, N, C), F32), V((MB, N, C), F32),
            V((N, 128), BF), V((2 * groups, 8, 128), F32),
            V((N, C + 128), BF), V((MB, N, 3 * C), BF),
            V((C, C), BF), V((C, C), BF), V((128, C), BF), V((128, C), BF), V((2, C, 128), BF),
            V((8, C), F32), V((4, 8, C), F32), V((C, 3 * C), F32),
            V((ND, PK, C), BF), V((ND, PK // 2, C), BF), V((ND, PK // 2, C), BF),
            V((ND, PK // 2, C), BF), V((PK // 2, C), BF), V((NG, PK // 2, C), BF),
            DMA((5,)), DMA((MB,)), DMA((MB, NCH)), DMA((MB,)), DMA((MB, NCH)),
            DMA((4,)), DMA((6,)), DMA((MB,)),
        ],
        compiler_params=pltpu.CompilerParams(
            collective_id=0, has_side_effects=True, vmem_limit_bytes=62 * 2**20
        ),
        cost_estimate=pl.CostEstimate(
            flops=20 * MB * E * N * C, bytes_accessed=10 * MB * N * C, transcendentals=4 * MB * E * C
        ),
    )(
        jnp.swapaxes(node_count, 0, 1), jnp.swapaxes(edge_src, 2, 3), jnp.swapaxes(edge_tgt, 2, 3),
        attention.reshape(1, RW), out_bias.reshape(1, RW), norm_gain.reshape(1, RW), norm_shift.reshape(1, RW),
        features, cotangent, w_source, w_target, w_residual,
    )
    outs = pl.pallas_call(
        functools.partial(hand_on, RW),
        out_shape=(wide, wide, block, block, block, line, line, line, line),
        in_specs=[hbm, hbm, vmem],
        out_specs=(hbm, hbm) + (vmem,) * 7,
        scratch_shapes=[V((2 * MB, N, C), BF), DMA((2, 2 * MB))],
    )(result, grad_rows, small)
    return outs[:5] + tuple(v.reshape(RW) for v in outs[5:])


def solution(mesh):
    shape = (mesh.shape["grp"], mesh.shape["dev"])
    return jax.shard_map(
        functools.partial(local, shape),
        mesh=mesh,
        in_specs=(
            P(None, ("grp", "dev"), None),
            P("dev", None),
            P("dev", None),
            P("dev", None),
            P("dev"),
            P("dev"),
            P("dev"),
            P("dev"),
            P(None, ("grp", "dev")),
            P(None, ("grp", "dev"), None, None),
            P(None, ("grp", "dev"), None, None),
            P(None, ("grp", "dev"), None),
        ),
        out_specs=(
            P(None, ("grp", "dev"), None),
            P(None, ("grp", "dev"), None),
            P("dev", None),
            P("dev", None),
            P("dev", None),
            P("dev"),
            P("dev"),
            P("dev"),
            P("dev"),
        ),
        check_vma=False,
    )
```
